32 devices in a mesh: row: 4 (over y, core), col: 8 (over z, x).
Axes of the slice: x: 2, y: 2, z: 4, core: 2. Of those that a mesh axis runs over, the one named last changes fastest.
Arguments:
- child_fronts: float32 [2, 8192, 8192], P(None, 'row', 'col'), may hold values from 0 to 50
- parent_entries: float32 [8192, 8192], P('row', 'col'), may hold values from 0 to 50, as said below
- block_map: int32 [2, 30], replicated, may hold values from 0 to 31, as said below
Outputs:
- child_factored: float32 [2, 8192, 8192], P(None, 'row', 'col')
- parent_factored: float32 [8192, 8192], P('row', 'col')
The draws below stay inside these ranges and needn't reach their ends.
Inputs may be any that keep to these rules, and one draw needn't show every extreme that they name: `parent_entries`: symmetric and positive definite. `block_map`: each row is strictly increasing, begins with 0, ends with 31 and never takes the value 30.
All inputs are finite; a program needn't handle non-finite values.
Results may differ from the reference program's by a relative error of at most 0.0003.
Values sent between devices are 32-bit elements; how exact they have to be, the bound alone decides.
No kernel may reach another device: no remote copies, remote signals or barrier semaphores. Data moves between devices by JAX's collectives and lax.ppermute only.
A program may use at most 192 MiB of HBM per device.

```python
import math
import jax
import jax.numpy as jnp
from jax import lax

NF = 8192
SEP = 512
BLK = 256
NB = 32
NCB = 30


kernel_range = 0.07


def kernel_front(key):
    keys = jax.random.split(key, 4)
    plane_x = jax.random.uniform(keys[0], (NF,), jnp.float32)
    plane_y = jax.random.uniform(keys[1], (NF,), jnp.float32)
    raw_depth = jax.random.uniform(keys[2], (NF,), jnp.float32)
    index_all = jnp.arange(NF)
    depth = jnp.where(index_all < SEP, 0.45 + 0.1 * raw_depth, raw_depth)
    scales = jnp.exp(jax.random.uniform(keys[3], (NF,), jnp.float32, math.log(0.5), math.log(5.0)))
    diff_x = plane_x[:, None] - plane_x[None, :]
    diff_y = plane_y[:, None] - plane_y[None, :]
    diff_z = depth[:, None] - depth[None, :]
    distance = jnp.sqrt(diff_x * diff_x + diff_y * diff_y + diff_z * diff_z)
    on_diagonal = (index_all[:, None] == index_all[None, :]).astype(jnp.float32)
    kernel = jnp.exp(-distance / kernel_range) + on_diagonal
    return kernel * (scales[:, None] * scales[None, :])


def draw_child_fronts(key, part):
    base = jax.random.fold_in(key, 11)
    return lax.map(kernel_front, jax.random.split(base, 2))


def draw_parent_entries(key, part):
    return kernel_front(jax.random.fold_in(key, 23))


def draw_block_map(key, part):
    base = jax.random.fold_in(key, 37)
    gap_count = SEP // BLK
    map_rows = []
    for child_index in range(2):
        shuffled = jax.random.permutation(jax.random.fold_in(base, child_index), NB - 3) + 1
        gaps = jnp.concatenate([shuffled[:gap_count - 1], jnp.array([NB - 2], jnp.int32)]).astype(jnp.int32)
        blocks = jnp.arange(NB)
        is_gap = jnp.any(blocks[:, None] == gaps[None, :], axis=1)
        present = jnp.where(is_gap, 0, 1).astype(jnp.int32)
        ranks = jnp.cumsum(present) - 1
        slots = jnp.arange(NCB)
        chosen = (ranks[None, :] == slots[:, None]) & (present[None, :] == 1)
        map_rows.append(jnp.sum(jnp.where(chosen, blocks[None, :], 0), axis=1).astype(jnp.int32))
    return jnp.stack(map_rows)


def setup_inputs(seed: int = 0) -> dict:
    arg_keys = jax.random.split(jax.random.key(seed), 4)
    child_fronts = draw_child_fronts(jax.random.fold_in(arg_keys[3], 71), 0)
    parent_entries = draw_parent_entries(jax.random.fold_in(arg_keys[3], 71), 0)
    block_map = draw_block_map(jax.random.fold_in(arg_keys[3], 71), 0)
    return dict(child_fronts=child_fronts, parent_entries=parent_entries, block_map=block_map)


def partial_factor(front_mat):
    pivot_block = front_mat[:SEP, :SEP]
    lower_factor = jnp.linalg.cholesky(pivot_block)
    factor_rows = jax.scipy.linalg.solve_triangular(lower_factor, front_mat[:SEP, :], lower=True)
    trailing = factor_rows[:, SEP:]
    schur_block = front_mat[SEP:, SEP:] - jnp.dot(trailing.T, trailing, precision=lax.Precision.HIGHEST)
    lower_part = jnp.concatenate([jnp.zeros((NF - SEP, SEP), jnp.float32), schur_block], axis=1)
    return (jnp.concatenate([factor_rows, lower_part], axis=0), schur_block)

def reference(child_fronts, parent_entries, block_map):
    first_out, first_schur = partial_factor(child_fronts[0])
    second_out, second_schur = partial_factor(child_fronts[1])
    assembled = parent_entries.reshape(NB, BLK, NB, BLK)
    for child_index, schur_block in ((0, first_schur), (1, second_schur)):
        blocks = schur_block.reshape(NCB, BLK, NCB, BLK).transpose(0, 2, 1, 3)
        targets = block_map[child_index].astype(jnp.int32)
        assembled = assembled.at[targets[:, None], :, targets[None, :], :].add(blocks)
    parent_out, parent_schur = partial_factor(assembled.reshape(NF, NF))
    return (jnp.stack([first_out, second_out]), parent_out)
```

```python
import jax
import jax.numpy as jnp
from jax import lax
from jax.experimental import pallas as pl
from jax.experimental.pallas import tpu as pltpu
from jax.sharding import PartitionSpec as P

SEP = 512
BLK = 256
GAP = SEP // BLK
DB = 128
SUB = 8
VMEM = 56 * 2**20
F32 = jnp.float32
BF16 = jnp.bfloat16


def split(value):
    high = value.astype(BF16)
    return high, (value - high.astype(F32)).astype(BF16)


def dot(a, b, dims=((1,), (0,)), precision=None):
    return lax.dot_general(a, b, (dims, ((), ())), precision=precision, preferred_element_type=F32)


def dot3(a, b, dims=((1,), (0,))):
    return dot(a[0], b[0], dims) + (dot(a[0], b[1], dims) + dot(a[1], b[0], dims))


def dot_full(a, b, dims=((1,), (0,))):
    return dot(a, b, dims, lax.Precision.HIGHEST)


def factor_diag(tiles):
    shape = tiles[0][0].shape
    sub_iota = lax.broadcasted_iota(jnp.int32, shape, 1)
    left = [tile[0] for tile in tiles]
    right = [tile[1] for tile in tiles]
    done = []

    def row(tile, k):
        return jnp.broadcast_to(tile[:, k : k + 1, :], shape)

    for t in range(len(tiles)):
        first = t * SUB

        def lanes(tile, k, first=first):
            return jnp.broadcast_to(tile[:, :, first + k : first + k + 1], shape)

        cols = [lanes(left[t], k) for k in range(SUB)]
        a = [[row(cols[k], i) for k in range(i + 1)] for i in range(SUB)]
        inv = [None] * SUB
        low = [[None] * SUB for _ in range(SUB)]
        for j in range(SUB):
            inv[j] = lax.rsqrt(a[j][j])
            for i in range(j + 1, SUB):
                low[i][j] = a[i][j] * inv[j]
            for i in range(j + 1, SUB):
                for k in range(j + 1, i + 1):
                    a[i][k] = a[i][k] - low[i][j] * low[k][j]
        m = [[None] * SUB for _ in range(SUB)]
        for j in range(SUB):
            m[j][j] = inv[j]
            for i in range(j + 1, SUB):
                total = low[i][j] * m[j][j]
                for k in range(j + 1, i):
                    total = total + low[i][k] * m[k][j]
                m[i][j] = -inv[i] * total
        mcol = []
        for k in range(SUB):
            vec = jnp.zeros(shape, F32)
            for i in range(k, SUB):
                vec = jnp.where(sub_iota == i, m[i][k], vec)
            mcol.append(vec)
        new_left = mcol[0] * row(left[t], 0)
        new_right = mcol[0] * row(right[t], 0)
        for k in range(1, SUB):
            new_left = new_left + mcol[k] * row(left[t], k)
            new_right = new_right + mcol[k] * row(right[t], k)
        done.append(new_right)
        rows_left = [row(new_left, i) for i in range(SUB)]
        rows_right = [row(new_right, i) for i in range(SUB)]
        for s in range(t + 1, len(tiles)):
            raw = [lanes(left[s], k) for k in range(SUB)]
            for i in range(SUB):
                g = m[i][0] * raw[0]
                for k in range(1, i + 1):
                    g = g + m[i][k] * raw[k]
                left[s] = left[s] - g * rows_left[i]
                right[s] = right[s] - g * rows_right[i]
    return done


def chol_steps(work, diag, inv_ref, invt_ref):
    count = work.shape[0]
    steps = SEP // DB
    eye = (
        lax.broadcasted_iota(jnp.int32, (DB, DB), 0) == lax.broadcasted_iota(jnp.int32, (DB, DB), 1)
    ).astype(F32)
    for b in range(count):
        for k in range(steps):
            for j in range(steps):
                work[b, pl.ds(k * DB, DB), pl.ds(SEP + j * DB, DB)] = eye if j == k else jnp.zeros((DB, DB), F32)

    def step(k, carry):
        rows = pl.ds(pl.multiple_of(k * DB, DB), DB)
        for b in range(count):
            diag[b] = work[b, rows, rows]
        tiles = []
        for t in range(DB // SUB):
            unit = jnp.broadcast_to(eye[t * SUB : (t + 1) * SUB, :][None], (count, SUB, DB))
            tiles.append((diag[:, pl.ds(t * SUB, SUB), :], unit))
        outs = factor_diag(tiles)
        for t in range(DB // SUB):
            diag[:, pl.ds(t * SUB, SUB), :] = outs[t]
        for b in range(count):
            work[b, rows, :] = dot_full(diag[b], work[b, rows, :])

        def update(i, c):
            irows = pl.ds(pl.multiple_of(i * DB, DB), DB)
            for b in range(count):
                work[b, irows, :] = work[b, irows, :] - dot_full(work[b, rows, irows], work[b, rows, :], ((0,), (0,)))
            return c

        lax.fori_loop(k + 1, steps, update, 0)
        return carry

    lax.fori_loop(0, steps, step, 0)
    for b in range(count):
        inv = work[b, :, pl.ds(SEP, SEP)]
        inv_ref[b] = inv
        invt_ref[b] = inv.T


def call(kernel, grid, in_specs, out_shape, out_specs, scratch, args, flops, nbytes, aliases=None):
    return pl.pallas_call(
        kernel,
        out_shape=out_shape,
        grid_spec=pltpu.PrefetchScalarGridSpec(
            num_scalar_prefetch=1, grid=grid, in_specs=in_specs, out_specs=out_specs, scratch_shapes=scratch
        ),
        input_output_aliases=aliases or {},
        compiler_params=pltpu.CompilerParams(vmem_limit_bytes=VMEM),
        cost_estimate=pl.CostEstimate(flops=int(flops), bytes_accessed=int(nbytes), transcendentals=0),
    )(*args)


def shape_of(dims, dtype=F32):
    return jax.ShapeDtypeStruct(dims, dtype)


class Plan:
    def __init__(self, rows, cols, rows_loc, cols_loc):
        self.rows, self.cols, self.rows_loc, self.cols_loc = rows, cols, rows_loc, cols_loc
        self.row_blocks, self.col_blocks = rows_loc // BLK, cols_loc // BLK
        self.blocks = rows * rows_loc // BLK
        self.half = cols_loc // SEP
        assert cols == 2 * rows and rows_loc == 2 * cols_loc and rows_loc >= 2 * SEP and cols_loc >= SEP

    def r(self, s):
        return s[2 * self.blocks]

    def c(self, s):
        return s[2 * self.blocks + 1]

    def source(self, s, k, block):
        return s[k * self.blocks + block]

    def row_at(self, s, k, i):
        found = self.source(s, k, self.r(s) * self.row_blocks + i)
        return found >= 0, jnp.where(found >= 0, found - self.r(s) * self.row_blocks, 0)

    def col_at(self, s, k, j):
        found = self.source(s, k, self.c(s) * self.col_blocks + j)
        return found >= 0, jnp.where(found >= 0, found - self.c(s) * self.col_blocks, 0)

    def before_at(self, s, k, j):
        start = self.c(s) * self.col_blocks
        found = self.source(s, k, jnp.maximum(start - GAP + j, 0)) - start
        valid = (found >= 0) & (start > 0)
        return valid, jnp.where(valid, found, 0)


def child_factor(plan, scal, head_a, head_b):
    def kernel(s, a_ref, b_ref, inv_ref, invt_ref, work, diag):
        work[0, :, pl.ds(0, SEP)] = a_ref[...]
        work[1, :, pl.ds(0, SEP)] = b_ref[...]
        chol_steps(work, diag, inv_ref, invt_ref)

    block = pl.BlockSpec((SEP, SEP), lambda g, s: (0, 0))
    out = pl.BlockSpec((2, SEP, SEP), lambda g, s: (0, 0, 0))
    return call(
        kernel, (1,), [block, block], [shape_of((2, SEP, SEP))] * 2, [out, out],
        [pltpu.VMEM((2, SEP, 2 * SEP), F32), pltpu.VMEM((2, DB, DB), F32)],
        (scal, head_a, head_b), 3e10, 6 * 2**20,
    )


def parent_factor(plan, scal, pivot, rt, cols):
    def kernel(s, p_ref, ah, al, bh, bl, cah, cal, cbh, cbl, inv_ref, invt_ref, work, diag):
        total = p_ref[...]
        for k, (lh, ll, rh, rl) in enumerate(((ah, al, cah, cal), (bh, bl, cbh, cbl))):
            update = dot3((lh[...], ll[...]), (rh[...], rl[...]))
            keep = plan.source(s, k, 1) >= 0
            edge = lax.broadcasted_iota(jnp.int32, (SEP, SEP), 0) >= BLK
            edge = edge | (lax.broadcasted_iota(jnp.int32, (SEP, SEP), 1) >= BLK)
            total = total - jnp.where(edge & jnp.logical_not(keep), 0.0, update)
        work[0, :, pl.ds(0, SEP)] = total
        chol_steps(work, diag, inv_ref, invt_ref)

    pivot_spec = pl.BlockSpec((SEP, SEP), lambda g, s: (0, 0))
    left = pl.BlockSpec((SEP, SEP), lambda g, s: (2 * plan.half + 1, 0))
    right = pl.BlockSpec((SEP, SEP), lambda g, s: (0, plan.half + 1))
    out = pl.BlockSpec((1, SEP, SEP), lambda g, s: (0, 0, 0))
    return call(
        kernel, (1,), [pivot_spec] + [left] * 4 + [right] * 4, [shape_of((1, SEP, SEP))] * 2, [out, out],
        [pltpu.VMEM((1, SEP, 2 * SEP), F32), pltpu.VMEM((1, DB, DB), F32)],
        (scal, pivot, *rt[0], *rt[1], *cols[0], *cols[1]), 2.5e10, 6 * 2**20,
    )


def child_rows(plan, scal, k, own, other, after, head, invt):
    half = plan.half
    jobs = 2 * half + 2

    def kernel(s, o_ref, e_ref, x_ref, h_ref, l_ref, hi_ref, lo_ref, lh, ll):
        j = pl.program_id(0)

        @pl.when(j == 0)
        def _():
            lh[...], ll[...] = split(l_ref[0])

        side = j // half
        parity = plan.c(s) % 2
        value = jnp.where(side == parity, o_ref[...], e_ref[...])
        value = jnp.where(j == 2 * half, x_ref[...], jnp.where(j == 2 * half + 1, h_ref[...], value))
        hi_ref[...], lo_ref[...] = split(dot3(split(value), (lh[...], ll[...])))

    def own_at(j, s):
        return (jnp.clip(j - half * (plan.c(s) % 2), 0, half - 1), 0)

    def other_at(j, s):
        return (jnp.clip(j - half * (1 - plan.c(s) % 2), 0, half - 1), 0)

    blk = (SEP, SEP)
    out = pl.BlockSpec(blk, lambda j, s: (j, 0))
    return call(
        kernel, (jobs,),
        [pl.BlockSpec(blk, own_at), pl.BlockSpec(blk, other_at), pl.BlockSpec(blk, lambda j, s: (0, 0)),
         pl.BlockSpec(blk, lambda j, s: (1, 0)), pl.BlockSpec((1, SEP, SEP), lambda j, s: (k, 0, 0))],
        [shape_of((jobs * SEP, SEP), BF16)] * 2, [out, out], [pltpu.VMEM(blk, BF16)] * 2,
        (scal, own, other, after, head, invt), 6 * jobs * SEP**3, 8 * jobs * SEP**2,
    )


def child_cols(plan, scal, k, own, after, head, inv):
    half = plan.half
    jobs = half + 2

    def kernel(s, o_ref, x_ref, h_ref, l_ref, hi_ref, lo_ref, lh, ll):
        j = pl.program_id(0)

        @pl.when(j == 0)
        def _():
            lh[...], ll[...] = split(l_ref[0])

        @pl.when(j <= half)
        def _():
            value = jnp.where(j == half, x_ref[...], o_ref[...])
            hi_ref[...], lo_ref[...] = split(dot3((lh[...], ll[...]), split(value)))

        @pl.when(j == half + 1)
        def _():
            hi_ref[...], lo_ref[...] = split(dot3((lh[...], ll[...]), split(h_ref[...]), ((1,), (1,))))

    blk = (SEP, SEP)
    out = pl.BlockSpec(blk, lambda j, s: (0, j))
    return call(
        kernel, (jobs,),
        [pl.BlockSpec(blk, lambda j, s: (0, jnp.minimum(j, half - 1))), pl.BlockSpec(blk, lambda j, s: (0, 0)),
         pl.BlockSpec(blk, lambda j, s: (1, 0)), pl.BlockSpec((1, SEP, SEP), lambda j, s: (k, 0, 0))],
        [shape_of((SEP, jobs * SEP), BF16)] * 2, [out, out], [pltpu.VMEM(blk, BF16)] * 2,
        (scal, own, after, head, inv), 6 * jobs * SEP**3, 8 * jobs * SEP**2,
    )


def parent_rows(plan, scal, own, other, rt, cols, invt):
    count = plan.row_blocks
    in_half = count // 2

    def kernel(s, o_ref, e_ref, ah, al, bh, bl, cah, cal, cbh, cbl, l_ref, hi_ref, lo_ref, lh, ll, rh, rl):
        i = pl.program_id(0)

        @pl.when(i == 0)
        def _():
            lh[...], ll[...] = split(l_ref[0])
            for k, (high, low) in enumerate(((cah, cal), (cbh, cbl))):
                keep = plan.source(s, k, 1) >= 0
                lane = lax.broadcasted_iota(jnp.int32, (SEP, SEP), 1)
                drop = (lane >= BLK) & jnp.logical_not(keep)
                rh[k] = jnp.where(drop, 0.0, high[...].astype(F32)).astype(BF16)
                rl[k] = jnp.where(drop, 0.0, low[...].astype(F32)).astype(BF16)

        side = i // in_half
        value = jnp.where(side == plan.c(s) % 2, o_ref[...], e_ref[...])
        for k, (high, low) in enumerate(((ah, al), (bh, bl))):
            valid, _ = plan.row_at(s, k, i)
            value = value - jnp.where(valid, dot3((high[...], low[...]), (rh[k], rl[k])), 0.0)
        hi_ref[...], lo_ref[...] = split(dot3(split(value), (lh[...], ll[...])))

    def own_at(i, s):
        return (jnp.clip(i - in_half * (plan.c(s) % 2), 0, in_half - 1), 0)

    def other_at(i, s):
        return (jnp.clip(i - in_half * (1 - plan.c(s) % 2), 0, in_half - 1), 0)

    blk = (BLK, SEP)
    rows = [pl.BlockSpec(blk, lambda i, s, k=k: (plan.row_at(s, k, i)[1], 0)) for k in (0, 0, 1, 1)]
    head = pl.BlockSpec((SEP, SEP), lambda i, s: (0, plan.half + 1))
    out = pl.BlockSpec(blk, lambda i, s: (i, 0))
    return call(
        kernel, (count,),
        [pl.BlockSpec(blk, own_at), pl.BlockSpec(blk, other_at)] + rows + [head] * 4
        + [pl.BlockSpec((1, SEP, SEP), lambda i, s: (0, 0, 0))],
        [shape_of((plan.rows_loc, SEP), BF16)] * 2, [out, out],
        [pltpu.VMEM((SEP, SEP), BF16)] * 2 + [pltpu.VMEM((2, SEP, SEP), BF16)] * 2,
        (scal, own, other, *rt[0], *rt[1], *cols[0], *cols[1], invt),
        18 * plan.rows_loc * SEP**2, 16 * plan.rows_loc * SEP,
    )


def parent_cols(plan, scal, panel, rt, cols, inv):
    count = plan.col_blocks

    def kernel(s, p_ref, ah, al, bh, bl, cah, cal, cbh, cbl, l_ref, hi_ref, lo_ref, lh, ll, rh, rl):
        j = pl.program_id(0)

        @pl.when(j == 0)
        def _():
            lh[...], ll[...] = split(l_ref[0])
            for k, (high, low) in enumerate(((ah, al), (bh, bl))):
                keep = plan.source(s, k, 1) >= 0
                line = lax.broadcasted_iota(jnp.int32, (SEP, SEP), 0)
                drop = (line >= BLK) & jnp.logical_not(keep)
                rh[k] = jnp.where(drop, 0.0, high[...].astype(F32)).astype(BF16)
                rl[k] = jnp.where(drop, 0.0, low[...].astype(F32)).astype(BF16)

        value = p_ref[...]
        for k, (high, low) in enumerate(((cah, cal), (cbh, cbl))):
            valid, _ = plan.col_at(s, k, j)
            value = value - jnp.where(valid, dot3((rh[k], rl[k]), (high[...], low[...])), 0.0)
        hi_ref[...], lo_ref[...] = split(dot3((lh[...], ll[...]), split(value)))

    blk = (SEP, BLK)
    head = pl.BlockSpec((SEP, SEP), lambda j, s: (2 * plan.half + 1, 0))
    right = [pl.BlockSpec(blk, lambda j, s, k=k: (0, plan.col_at(s, k, j)[1])) for k in (0, 0, 1, 1)]
    out = pl.BlockSpec(blk, lambda j, s: (0, j))
    return call(
        kernel, (count,),
        [out] + [head] * 4 + right + [pl.BlockSpec((1, SEP, SEP), lambda j, s: (0, 0, 0))],
        [shape_of((SEP, plan.cols_loc), BF16)] * 2, [out, out],
        [pltpu.VMEM((SEP, SEP), BF16)] * 2 + [pltpu.VMEM((2, SEP, SEP), BF16)] * 2,
        (scal, panel, *rt[0], *rt[1], *cols[0], *cols[1], inv),
        18 * plan.cols_loc * SEP**2, 16 * plan.cols_loc * SEP,
    )


def child_result(plan, scal, k, fronts, rt, cols, result):
    wide = plan.cols_loc

    def kernel(s, a_ref, lh, ll, rh, rl, *rest):
        out_ref = rest[-1]
        i = pl.program_id(0)
        top = (plan.r(s) == 0) & (i < GAP)

        @pl.when(top)
        def _():
            rows = pl.ds(pl.multiple_of(jnp.minimum(i, GAP - 1) * BLK, BLK), BLK)
            out_ref[0] = rh[rows, :].astype(F32) + rl[rows, :].astype(F32)

        @pl.when(jnp.logical_not(top))
        def _():
            out_ref[0] = a_ref[0] - dot3((lh[...], ll[...]), (rh[...], rl[...]))

            @pl.when(plan.c(s) == 0)
            def _():
                out_ref[0, :, pl.ds(0, SEP)] = jnp.zeros((BLK, SEP), F32)

    block = pl.BlockSpec((1, BLK, wide), lambda i, s: (k, i, 0))
    left = pl.BlockSpec((BLK, SEP), lambda i, s: (i, 0))
    right = pl.BlockSpec((SEP, wide), lambda i, s: (0, 0))
    extra_specs = [] if result is None else [pl.BlockSpec(memory_space=pl.ANY)]
    extra = [] if result is None else [result]
    return call(
        kernel, (plan.row_blocks,), [block, left, left, right, right] + extra_specs,
        shape_of(fronts.shape), block, [], (scal, fronts, *rt, *cols, *extra),
        6 * plan.rows_loc * wide * SEP, 8 * plan.rows_loc * wide,
        aliases={} if result is None else {6: 0},
    )


def edge_sum(plan, scal, fronts, after, first, count):
    last = plan.row_blocks - 1
    inner = after is None

    def kernel(s, a_ref, b_ref, *rest):
        out_ref = rest[-1]
        i = pl.program_id(0) + first
        for j in range(GAP):
            total = jnp.zeros((BLK, BLK), F32)
            for k, ref in enumerate((a_ref, b_ref)):
                valid_row, at_row = plan.row_at(s, k, i)
                valid_col, at_col = plan.before_at(s, k, j)
                lanes = pl.ds(pl.multiple_of(at_col * BLK, BLK), BLK)
                value = ref[0, :, lanes]
                if not inner:
                    value = jnp.where(at_row > last, rest[k][0, :, lanes], value)
                total = total + jnp.where(valid_row & valid_col, value, 0.0)
            out_ref[:, pl.ds(j * BLK, BLK)] = total

    blk = (1, BLK, SEP)
    own = [pl.BlockSpec(blk, lambda g, s, k=k: (k, jnp.minimum(plan.row_at(s, k, g + first)[1], last), 0)) for k in (0, 1)]
    ext = [
        pl.BlockSpec(blk, lambda g, s, k=k: (k, jnp.clip(plan.row_at(s, k, g + first)[1] - last - 1, 0, GAP - 1), 0))
        for k in (0, 1)
    ]
    return call(
        kernel, (count,), own + ([] if inner else ext), shape_of((count * BLK, SEP)),
        pl.BlockSpec((BLK, SEP), lambda g, s: (g, 0)), [],
        (scal, fronts, fronts) + (() if inner else (after, after)), 1e6, 16 * count * BLK * SEP,
    )


def add_entries(plan, s, i, total_ref, refs, ext_refs, edge_ref, out_wide):
    last = plan.row_blocks - 1
    for k in (0, 1):
        valid_row, at_row = plan.row_at(s, k, i)
        for j in range(plan.col_blocks):
            valid_col, at_col = plan.col_at(s, k, j)
            here = valid_row & valid_col & (at_col < plan.col_blocks)

            @pl.when(here)
            def _(k=k, j=j, at_col=at_col, at_row=at_row):
                lanes = pl.ds(pl.multiple_of(at_col * BLK, BLK), BLK)
                value = refs[k][0, :, lanes]
                if ext_refs is not None:
                    value = jnp.where(at_row > last, ext_refs[k][0, :, lanes], value)
                total_ref[:, pl.ds(j * BLK, BLK)] += value

    @pl.when(plan.c(s) < plan.cols - 1)
    def _():
        total_ref[:, pl.ds(out_wide - SEP, SEP)] += edge_ref[...]


def panel_start(plan, scal, entries, fronts, edge):
    wide = plan.cols_loc

    def kernel(s, e_ref, a_ref, b_ref, x_ref, out_ref):
        out_ref[...] = e_ref[...]
        add_entries(plan, s, pl.program_id(0), out_ref, (a_ref, b_ref), None, x_ref, wide)

    blk = (BLK, wide)
    own = [
        pl.BlockSpec((1, BLK, wide), lambda g, s, k=k: (k, plan.row_at(s, k, g)[1], 0)) for k in (0, 1)
    ]
    here = pl.BlockSpec(blk, lambda g, s: (g, 0))
    return call(
        kernel, (GAP,), [here] + own + [pl.BlockSpec((BLK, SEP), lambda g, s: (g, 0))],
        shape_of((SEP, wide)), here, [], (scal, entries, fronts, fronts, edge), 1e6, 16 * SEP * wide,
    )


def parent_result(plan, scal, entries, fronts, after, edge_top, edge_rest, rt, cols, prt, pcols):
    wide = plan.cols_loc
    last = plan.row_blocks - 1
    lhs_blk = (BLK, SEP)

    def kernel(s, e_ref, a_ref, b_ref, xa_ref, xb_ref, t_ref, u_ref, ah, al, bh, bl, ph, pll, cah, cal, cbh, cbl,
               qh, ql, out_ref, rh, rl, edge):
        i = pl.program_id(0)
        top = (plan.r(s) == 0) & (i < GAP)

        @pl.when(i == 0)
        def _():
            for k, (high, low) in enumerate(((cah, cal), (cbh, cbl))):
                for j in range(plan.col_blocks):
                    valid, at = plan.col_at(s, k, j)
                    lanes = pl.ds(pl.multiple_of(at * BLK, BLK), BLK)
                    here = pl.ds(j * BLK, BLK)
                    rh[k, :, here] = jnp.where(valid, high[:, lanes].astype(F32), 0.0).astype(BF16)
                    rl[k, :, here] = jnp.where(valid, low[:, lanes].astype(F32), 0.0).astype(BF16)

        @pl.when(top)
        def _():
            rows = pl.ds(pl.multiple_of(jnp.minimum(i, GAP - 1) * BLK, BLK), BLK)
            out_ref[...] = qh[rows, :].astype(F32) + ql[rows, :].astype(F32)

        @pl.when(jnp.logical_not(top))
        def _():
            out_ref[...] = e_ref[...] - dot3((ph[...], pll[...]), (qh[...], ql[...]))
            for k, (high, low) in enumerate(((ah, al), (bh, bl))):
                valid, _ = plan.row_at(s, k, i)

                @pl.when(valid)
                def _(k=k, high=high, low=low):
                    out_ref[...] -= dot3((high[...], low[...]), (rh[k], rl[k]))

            edge[...] = jnp.where(i < GAP, t_ref[...], u_ref[...])
            add_entries(plan, s, i, out_ref, (a_ref, b_ref), (xa_ref, xb_ref), edge, wide)

            @pl.when(plan.c(s) == 0)
            def _():
                out_ref[:, pl.ds(0, SEP)] = jnp.zeros((BLK, SEP), F32)

    here = pl.BlockSpec((BLK, wide), lambda g, s: (g, 0))
    front = (1, BLK, wide)
    own = [pl.BlockSpec(front, lambda g, s, k=k: (k, jnp.minimum(plan.row_at(s, k, g)[1], last), 0)) for k in (0, 1)]
    ext = [
        pl.BlockSpec(front, lambda g, s, k=k: (k, jnp.clip(plan.row_at(s, k, g)[1] - last - 1, 0, GAP - 1), 0))
        for k in (0, 1)
    ]
    top_spec = pl.BlockSpec(lhs_blk, lambda g, s: (jnp.minimum(g, GAP - 1), 0))
    rest_spec = pl.BlockSpec(lhs_blk, lambda g, s: (jnp.maximum(g - GAP, 0), 0))
    rows = [pl.BlockSpec(lhs_blk, lambda g, s, k=k: (plan.row_at(s, k, g)[1], 0)) for k in (0, 0, 1, 1)]
    prow = pl.BlockSpec(lhs_blk, lambda g, s: (g, 0))
    right = pl.BlockSpec((SEP, wide + SEP), lambda g, s: (0, 0))
    pright = pl.BlockSpec((SEP, wide), lambda g, s: (0, 0))
    return call(
        kernel, (plan.row_blocks,),
        [here] + own + ext + [top_spec, rest_spec] + rows + [prow] * 2 + [right] * 4 + [pright] * 2,
        shape_of((plan.rows_loc, wide)), here,
        [pltpu.VMEM((2, SEP, wide), BF16)] * 2 + [pltpu.VMEM(lhs_blk, F32)],
        (scal, entries, fronts, fronts, after, after, edge_top, edge_rest, *rt[0], *rt[1], *prt, *cols[0], *cols[1], *pcols),
        18 * plan.rows_loc * wide * SEP, 24 * plan.rows_loc * wide,
    )


def send(plan, value, pairs):
    flat = [(a * plan.cols + b, c * plan.cols + d) for (a, b), (c, d) in pairs]
    return lax.ppermute(value, ("row", "col"), flat)


def grid_of(plan):
    return [(a, b) for a in range(plan.rows) for b in range(plan.cols)]


def row_broadcast(plan, r, value):
    stride = plan.rows // 2
    while stride:
        sent = send(plan, value, [((a, b), (a + stride, b)) for a, b in grid_of(plan) if a % (2 * stride) == 0])
        value = jnp.where(r % (2 * stride) == stride, sent, value)
        stride //= 2
    return value


def from_next_row(plan, value):
    return send(plan, value, [((a + 1, b), (a, b)) for a, b in grid_of(plan) if a + 1 < plan.rows])


def from_next_col(plan, value):
    return send(plan, value, [((a, b + 1), (a, b)) for a, b in grid_of(plan) if b + 1 < plan.cols])


def swap_cols(plan, value):
    return send(plan, value, [((a, b), (a, b ^ 1)) for a, b in grid_of(plan)])


def swap_rows(plan, value):
    return send(plan, value, [((a, b), (a ^ 1, b)) for a, b in grid_of(plan)])


def spread(plan, r, c, value):
    place = c // 2
    up = send(plan, value, [((a, b), (a, b + 2)) for a, b in grid_of(plan) if b // 2 == a and b + 2 < plan.cols])
    down = send(plan, value, [((a, b), (a, b - 2)) for a, b in grid_of(plan) if b // 2 == a and b >= 2])
    now = jnp.where(place > r, up, down)
    out = jnp.where(place == r, value, now)
    for step in range(2, plan.rows):
        pairs = []
        for a, b in grid_of(plan):
            if b // 2 == a + step - 1 and b + 2 < plan.cols:
                pairs.append(((a, b), (a, b + 2)))
            if b // 2 == a - step + 1 and b >= 2:
                pairs.append(((a, b), (a, b - 2)))
        now = send(plan, now, pairs)
        out = jnp.where(jnp.abs(place - r) == step, now, out)
    return out


def lead(plan, c, own, other, count):
    if count <= plan.cols_loc:
        return jnp.where(c % 2 == 0, own[:count], other[:count])
    return jnp.where(c % 2 == 0, jnp.concatenate([own, other]), jnp.concatenate([other, own]))[:count]


def local(plan, child_fronts, parent_entries, block_map):
    r, c = lax.axis_index("row"), lax.axis_index("col")
    slots = jnp.arange(block_map.shape[1], dtype=jnp.int32)[None, None, :] + GAP
    targets = jnp.arange(plan.blocks, dtype=jnp.int32)[None, :, None]
    source = jnp.max(jnp.where(block_map[:, None, :] == targets, slots, -1), axis=2)
    scal = jnp.concatenate([source.reshape(-1), jnp.stack([r, c]).astype(jnp.int32)])

    edge_top = from_next_col(plan, edge_sum(plan, scal, child_fronts, None, 0, GAP))
    after_rows = from_next_row(plan, child_fronts[:, :SEP, :])

    panels, own, other, heads, next_rows = [], [], [], [], []
    for k in (0, 1):
        panel = row_broadcast(plan, r, child_fronts[k, :SEP, :])
        panels.append(panel)
        own.append(spread(plan, r, c, panel.T))
        other.append(swap_cols(plan, own[k]))
        heads.append(row_broadcast(plan, r, lead(plan, c, own[k], other[k], 2 * SEP)))
        next_rows.append(from_next_row(plan, lead(plan, c, own[k], other[k], SEP)))
    mine = from_next_col(plan, jnp.where(r % 2 == 0, panels[0][:, :SEP], panels[1][:, :SEP]))
    theirs = swap_rows(plan, mine)
    next_cols = [jnp.where(r % 2 == 0, mine, theirs), jnp.where(r % 2 == 0, theirs, mine)]

    panel = row_broadcast(plan, r, panel_start(plan, scal, parent_entries, child_fronts, edge_top))
    parent_own = spread(plan, r, c, panel.T)
    parent_other = swap_cols(plan, parent_own)
    pivot = row_broadcast(plan, r, lead(plan, c, parent_own, parent_other, SEP))

    edge_rest = from_next_col(
        plan, edge_sum(plan, scal, child_fronts, after_rows, GAP, plan.row_blocks - GAP)
    )

    inv, invt = child_factor(plan, scal, heads[0], heads[1])
    rt = [child_rows(plan, scal, k, own[k], other[k], next_rows[k], heads[k], invt) for k in (0, 1)]
    cols = [child_cols(plan, scal, k, panels[k], next_cols[k], heads[k], inv) for k in (0, 1)]
    result = child_result(plan, scal, 0, child_fronts, rt[0], cols[0], None)
    result = child_result(plan, scal, 1, child_fronts, rt[1], cols[1], result)

    pinv, pinvt = parent_factor(plan, scal, pivot, rt, cols)
    prt = parent_rows(plan, scal, parent_own, parent_other, rt, cols, pinvt)
    pcols = parent_cols(plan, scal, panel, rt, cols, pinv)
    parent = parent_result(
        plan, scal, parent_entries, child_fronts, after_rows, edge_top, edge_rest, rt, cols, prt, pcols
    )
    return (result, parent)


def solution(mesh):
    placed = (P(None, "row", "col"), P("row", "col"), P())

    def run(child_fronts, parent_entries, block_map):
        plan = Plan(mesh.shape["row"], mesh.shape["col"], child_fronts.shape[1], child_fronts.shape[2])
        return local(plan, child_fronts, parent_entries, block_map)

    return jax.shard_map(
        run,
        mesh=mesh,
        in_specs=placed,
        out_specs=(P(None, "row", "col"), P("row", "col")),
        check_vma=False,
    )
```

```python
import jax
import jax.numpy as jnp
from jax import lax
from jax.experimental import pallas as pl
from jax.experimental.pallas import tpu as pltpu
from jax.sharding import PartitionSpec as P

SEP = 512
BLK = 256
GAP = SEP // BLK
DB = 128
SUB = 8
VMEM = 56 * 2**20
F32 = jnp.float32
BF16 = jnp.bfloat16


def split(value):
    high = value.astype(BF16)
    return high, (value - high.astype(F32)).astype(BF16)


def dot(a, b, dims=((1,), (0,)), precision=None):
    return lax.dot_general(a, b, (dims, ((), ())), precision=precision, preferred_element_type=F32)


def dot3(a, b, dims=((1,), (0,))):
    return dot(a[0], b[0], dims) + (dot(a[0], b[1], dims) + dot(a[1], b[0], dims))


def dot_full(a, b, dims=((1,), (0,))):
    return dot(a, b, dims, lax.Precision.HIGHEST)


def factor_diag(tiles):
    shape = tiles[0][0].shape
    sub_iota = lax.broadcasted_iota(jnp.int32, shape, 1)
    left = [tile[0] for tile in tiles]
    right = [tile[1] for tile in tiles]
    done = []

    def row(tile, k):
        return jnp.broadcast_to(tile[:, k : k + 1, :], shape)

    for t in range(len(tiles)):
        first = t * SUB

        def lanes(tile, k, first=first):
            return jnp.broadcast_to(tile[:, :, first + k : first + k + 1], shape)

        cols = [lanes(left[t], k) for k in range(SUB)]
        a = [[row(cols[k], i) for k in range(i + 1)] for i in range(SUB)]
        inv = [None] * SUB
        low = [[None] * SUB for _ in range(SUB)]
        for j in range(SUB):
            inv[j] = lax.rsqrt(a[j][j])
            for i in range(j + 1, SUB):
                low[i][j] = a[i][j] * inv[j]
            for i in range(j + 1, SUB):
                for k in range(j + 1, i + 1):
                    a[i][k] = a[i][k] - low[i][j] * low[k][j]
        m = [[None] * SUB for _ in range(SUB)]
        for j in range(SUB):
            m[j][j] = inv[j]
            for i in range(j + 1, SUB):
                total = low[i][j] * m[j][j]
                for k in range(j + 1, i):
                    total = total + low[i][k] * m[k][j]
                m[i][j] = -inv[i] * total
        mcol = []
        for k in range(SUB):
            vec = jnp.zeros(shape, F32)
            for i in range(k, SUB):
                vec = jnp.where(sub_iota == i, m[i][k], vec)
            mcol.append(vec)
        new_left = mcol[0] * row(left[t], 0)
        new_right = mcol[0] * row(right[t], 0)
        for k in range(1, SUB):
            new_left = new_left + mcol[k] * row(left[t], k)
            new_right = new_right + mcol[k] * row(right[t], k)
        done.append(new_right)
        rows_left = [row(new_left, i) for i in range(SUB)]
        rows_right = [row(new_right, i) for i in range(SUB)]
        for s in range(t + 1, len(tiles)):
            raw = [lanes(left[s], k) for k in range(SUB)]
            for i in range(SUB):
                g = m[i][0] * raw[0]
                for k in range(1, i + 1):
                    g = g + m[i][k] * raw[k]
                left[s] = left[s] - g * rows_left[i]
                right[s] = right[s] - g * rows_right[i]
    return done


def pack_at(i, j):
    return i * (i + 1) // 2 + j


PACKED = pack_at(SEP // DB, 0) * DB


def unpack(ref, b, transposed, high_ref, low_ref):
    for i in range(SEP // DB):
        for j in range(SEP // DB):
            at = (pl.ds(j * DB, DB), pl.ds(i * DB, DB)) if transposed else (pl.ds(i * DB, DB), pl.ds(j * DB, DB))
            if j <= i:
                block = ref[b, pl.ds(pack_at(i, j) * DB, DB), :]
                high_ref[at], low_ref[at] = split(block.T if transposed else block)
            else:
                high_ref[at] = low_ref[at] = jnp.zeros((DB, DB), BF16)


def chol_steps(work, diag, inv_ref):
    count = work.shape[0]
    steps = SEP // DB
    eye = (
        lax.broadcasted_iota(jnp.int32, (DB, DB), 0) == lax.broadcasted_iota(jnp.int32, (DB, DB), 1)
    ).astype(F32)
    for b in range(count):
        for k in range(steps):
            for j in range(steps):
                work[b, pl.ds(k * DB, DB), pl.ds(SEP + j * DB, DB)] = eye if j == k else jnp.zeros((DB, DB), F32)

    def step(k, carry):
        rows = pl.ds(pl.multiple_of(k * DB, DB), DB)
        for b in range(count):
            diag[b] = work[b, rows, rows]
        tiles = []
        for t in range(DB // SUB):
            unit = jnp.broadcast_to(eye[t * SUB : (t + 1) * SUB, :][None], (count, SUB, DB))
            tiles.append((diag[:, pl.ds(t * SUB, SUB), :], unit))
        outs = factor_diag(tiles)
        for t in range(DB // SUB):
            diag[:, pl.ds(t * SUB, SUB), :] = outs[t]
        for b in range(count):
            work[b, rows, :] = dot_full(diag[b], work[b, rows, :])

        def update(i, c):
            irows = pl.ds(pl.multiple_of(i * DB, DB), DB)
            for b in range(count):
                work[b, irows, :] = work[b, irows, :] - dot_full(work[b, rows, irows], work[b, rows, :], ((0,), (0,)))
            return c

        lax.fori_loop(k + 1, steps, update, 0)
        return carry

    lax.fori_loop(0, steps, step, 0)
    for b in range(count):
        for i in range(steps):
            for j in range(i + 1):
                inv_ref[b, pl.ds(pack_at(i, j) * DB, DB), :] = work[b, pl.ds(i * DB, DB), pl.ds(SEP + j * DB, DB)]


def call(kernel, grid, in_specs, out_shape, out_specs, scratch, args, flops, nbytes, aliases=None):
    return pl.pallas_call(
        kernel,
        out_shape=out_shape,
        grid_spec=pltpu.PrefetchScalarGridSpec(
            num_scalar_prefetch=1, grid=grid, in_specs=in_specs, out_specs=out_specs, scratch_shapes=scratch
        ),
        input_output_aliases=aliases or {},
        compiler_params=pltpu.CompilerParams(vmem_limit_bytes=VMEM),
        cost_estimate=pl.CostEstimate(flops=int(flops), bytes_accessed=int(nbytes), transcendentals=0),
    )(*args)


def shape_of(dims, dtype=F32):
    return jax.ShapeDtypeStruct(dims, dtype)


class Plan:
    def __init__(self, rows, cols, rows_loc, cols_loc):
        self.rows, self.cols, self.rows_loc, self.cols_loc = rows, cols, rows_loc, cols_loc
        self.row_blocks, self.col_blocks = rows_loc // BLK, cols_loc // BLK
        self.blocks = rows * rows_loc // BLK
        self.half = cols_loc // SEP
        self.piece = cols_loc // rows
        assert cols == 2 * rows and rows_loc == 2 * cols_loc and rows_loc >= 2 * SEP and cols_loc >= SEP

    def r(self, s):
        return s[2 * self.blocks]

    def c(self, s):
        return s[2 * self.blocks + 1]

    def source(self, s, k, block):
        return s[k * self.blocks + block]

    def row_at(self, s, k, i):
        found = self.source(s, k, self.r(s) * self.row_blocks + i)
        return found >= 0, jnp.where(found >= 0, found - self.r(s) * self.row_blocks, 0)

    def col_at(self, s, k, j):
        found = self.source(s, k, self.c(s) * self.col_blocks + j)
        return found >= 0, jnp.where(found >= 0, found - self.c(s) * self.col_blocks, 0)

    def before_at(self, s, k, j):
        start = self.c(s) * self.col_blocks
        found = self.source(s, k, jnp.maximum(start - GAP + j, 0)) - start
        valid = (found >= 0) & (start > 0)
        return valid, jnp.where(valid, found, 0)


def pack_pivots(plan, scal, fronts, ahead):
    def kernel(s, a_ref, *rest):
        out_ref = rest[-1]
        for k in (0, 1):
            for i in range(SEP // DB):
                for j in range(i, SEP // DB):
                    block = a_ref[k, pl.ds(i * DB, DB), pl.ds(j * DB, DB)]
                    out_ref[k, pl.ds(pack_at(j, i) * DB, DB), :] = block

    return call(
        kernel, (1,),
        [pl.BlockSpec((2, SEP, SEP), lambda g, s: (0, 0, 0))] + [pl.BlockSpec(memory_space=pl.ANY)] * len(ahead),
        shape_of((2, PACKED, DB)), pl.BlockSpec((2, PACKED, DB), lambda g, s: (0, 0, 0)), [],
        (scal, fronts, *ahead), 1, 4 * 2**20,
    )


def child_factor(plan, scal, pivots, ahead):
    def kernel(s, a_ref, *rest):
        inv_ref, work, diag = rest[-3:]
        for k in (0, 1):
            for i in range(SEP // DB):
                for j in range(SEP // DB):
                    at = (k, pl.ds(i * DB, DB), pl.ds(j * DB, DB))
                    zero = jnp.zeros((DB, DB), F32)
                    work[at] = a_ref[k, pl.ds(pack_at(j, i) * DB, DB), :] if j >= i else zero
        chol_steps(work, diag, inv_ref)

    block = pl.BlockSpec((2, PACKED, DB), lambda g, s: (0, 0, 0))
    return call(
        kernel, (1,), [block] + [pl.BlockSpec(memory_space=pl.ANY)] * len(ahead), shape_of((2, PACKED, DB)), block,
        [pltpu.VMEM((2, SEP, 2 * SEP), F32), pltpu.VMEM((2, DB, DB), F32)], (scal, pivots, *ahead), 4e10, 4 * 2**20,
    )


def parent_factor(plan, scal, panel, wide, inv, ahead):
    def kernel(s, m_ref, p_ref, l_ref, *rest):
        out_ref, work, diag, full = rest[-4:]
        first = (plan.r(s) == 0) & (plan.c(s) == 0)

        @pl.when(first)
        def _():
            steps = SEP // DB
            total = m_ref[...]
            for k in (0, 1):
                for i in range(steps):
                    for j in range(steps):
                        zero = jnp.zeros((DB, DB), F32)
                        block = l_ref[k, pl.ds(pack_at(i, j) * DB, DB), :] if j <= i else zero
                        full[pl.ds(i * DB, DB), pl.ds(j * DB, DB)] = block
                head = dot_full(full[...], p_ref[k])
                update = dot_full(head, head, ((0,), (0,)))
                keep = plan.source(s, k, 1) >= 0
                edge = lax.broadcasted_iota(jnp.int32, (SEP, SEP), 0) >= BLK
                edge = edge | (lax.broadcasted_iota(jnp.int32, (SEP, SEP), 1) >= BLK)
                total = total - jnp.where(edge & jnp.logical_not(keep), 0.0, update)
            work[0, :, pl.ds(0, SEP)] = total
            chol_steps(work, diag, out_ref)

        @pl.when(jnp.logical_not(first))
        def _():
            out_ref[...] = jnp.zeros(out_ref.shape, F32)

    both = pl.BlockSpec((2, PACKED, DB), lambda g, s: (0, 0, 0))
    return call(
        kernel, (1,),
        [pl.BlockSpec((SEP, SEP), lambda g, s: (0, 0)), pl.BlockSpec((2, SEP, SEP), lambda g, s: (0, 0, 1)), both]
        + [pl.BlockSpec(memory_space=pl.ANY)] * len(ahead),
        shape_of((1, PACKED, DB)), pl.BlockSpec((1, PACKED, DB), lambda g, s: (0, 0, 0)),
        [pltpu.VMEM((1, SEP, 2 * SEP), F32), pltpu.VMEM((1, DB, DB), F32), pltpu.VMEM((SEP, SEP), F32)],
        (scal, panel, wide, inv, *ahead), 4e10, 8 * 2**20,
    )


def child_rows(plan, scal, k, rows, after, inv):
    count = plan.rows_loc // SEP
    slots = SEP // plan.piece

    def kernel(s, o_ref, x_ref, l_ref, hi_ref, lo_ref, lh, ll):
        j = pl.program_id(0)

        @pl.when(j == 0)
        def _():
            unpack(l_ref, 0, True, lh, ll)

        value = jnp.where(j == count, x_ref[...].reshape(SEP, SEP), o_ref[...].reshape(SEP, SEP))
        hi_ref[...], lo_ref[...] = split(dot3(split(value), (lh[...], ll[...])))

    blk = (SEP, SEP)
    cut = (slots, 1, 1, plan.piece, SEP)
    out = pl.BlockSpec(blk, lambda j, s: (j, 0))

    def own_at(j, s):
        at = jnp.minimum(j, count - 1)
        return (at % plan.half, at // plan.half, k, 0, 0)

    return call(
        kernel, (count + 1,),
        [pl.BlockSpec(cut, own_at), pl.BlockSpec(cut[:1] + cut[2:], lambda j, s: (0, k, 0, 0)),
         pl.BlockSpec((1, PACKED, DB), lambda j, s: (k, 0, 0))],
        [shape_of(((count + 1) * SEP, SEP), BF16)] * 2, [out, out], [pltpu.VMEM(blk, BF16)] * 2,
        (scal, rows, after, inv), 6 * (count + 1) * SEP**3, 8 * (count + 1) * SEP**2,
    )


def child_heads(plan, scal, head, inv):
    slots = SEP // plan.piece

    def kernel(s, h_ref, l_ref, hi_ref, lo_ref, thi_ref, tlo_ref, lh, ll):
        unpack(l_ref, 0, False, lh, ll)
        value = split(h_ref[...].reshape(SEP, SEP))
        out = dot3((lh[...], ll[...]), value, ((1,), (1,)))
        hi_ref[0], lo_ref[0] = split(out)
        thi_ref[0], tlo_ref[0] = split(out.T)

    out = pl.BlockSpec((1, SEP, SEP), lambda k, s: (k, 0, 0))
    return call(
        kernel, (2,),
        [pl.BlockSpec((slots, 1, plan.piece, SEP), lambda k, s: (0, k, 0, 0)),
         pl.BlockSpec((1, PACKED, DB), lambda k, s: (k, 0, 0))],
        [shape_of((2, SEP, SEP), BF16)] * 4, [out] * 4, [pltpu.VMEM((SEP, SEP), BF16)] * 2,
        (scal, head, inv), 12 * SEP**3, 16 * SEP**2,
    )


def child_cols(plan, scal, k, held, sent, inv):
    count = plan.half + 1

    def kernel(s, h_ref, t_ref, l_ref, hi_ref, lo_ref, lh, ll):
        @pl.when(pl.program_id(0) == 0)
        def _():
            unpack(l_ref, 0, False, lh, ll)

        value = jnp.where(plan.r(s) % 2 == 1, t_ref[0], h_ref[0])
        hi_ref[...], lo_ref[...] = split(dot3((lh[...], ll[...]), split(value)))

    blk = (SEP, SEP)
    out = pl.BlockSpec(blk, lambda j, s: (0, j))
    return call(
        kernel, (count,),
        [pl.BlockSpec((1, SEP, SEP), lambda j, s: (k, 0, jnp.where(plan.r(s) % 2 == 1, 0, j))),
         pl.BlockSpec((1, SEP, SEP), lambda j, s: (k, 0, jnp.where(plan.r(s) % 2 == 1, j, 0))),
         pl.BlockSpec((1, PACKED, DB), lambda j, s: (k, 0, 0))],
        [shape_of((SEP, count * SEP), BF16)] * 2, [out, out], [pltpu.VMEM(blk, BF16)] * 2,
        (scal, held, sent, inv), 6 * count * SEP**3, 8 * count * SEP**2,
    )


def parent_rows(plan, scal, panel, rt, heads, inv):
    count = plan.row_blocks

    def kernel(s, o_ref, ah, al, bh, bl, ch, cl, l_ref, hi_ref, lo_ref, lh, ll, rh, rl):
        i = pl.program_id(0)

        @pl.when(i == 0)
        def _():
            unpack(l_ref, 0, True, lh, ll)
            for k in (0, 1):
                keep = plan.source(s, k, 1) >= 0
                drop = (lax.broadcasted_iota(jnp.int32, (SEP, SEP), 1) >= BLK) & jnp.logical_not(keep)
                rh[k] = jnp.where(drop, 0.0, ch[k].astype(F32)).astype(BF16)
                rl[k] = jnp.where(drop, 0.0, cl[k].astype(F32)).astype(BF16)

        value = o_ref[...].reshape(BLK, SEP)
        for k, (high, low) in enumerate(((ah, al), (bh, bl))):
            valid, _ = plan.row_at(s, k, i)
            value = value - jnp.where(valid, dot3((high[...], low[...]), (rh[k], rl[k])), 0.0)
        hi_ref[...], lo_ref[...] = split(dot3(split(value), (lh[...], ll[...])))

    blk = (BLK, SEP)
    slots = BLK // plan.piece
    in_panel = count // 2
    own = pl.BlockSpec((slots, 1, plan.piece, SEP), lambda i, s: (i % in_panel, i // in_panel, 0, 0))
    rows = [pl.BlockSpec(blk, lambda i, s, k=k: (plan.row_at(s, k, i)[1], 0)) for k in (0, 0, 1, 1)]
    head = pl.BlockSpec((2, SEP, SEP), lambda i, s: (0, 0, 0))
    out = pl.BlockSpec(blk, lambda i, s: (i, 0))
    return call(
        kernel, (count,), [own] + rows + [head] * 2 + [pl.BlockSpec((1, PACKED, DB), lambda i, s: (0, 0, 0))],
        [shape_of((plan.rows_loc, SEP), BF16)] * 2, [out, out],
        [pltpu.VMEM((SEP, SEP), BF16)] * 2 + [pltpu.VMEM((2, SEP, SEP), BF16)] * 2,
        (scal, panel, *rt[0], *rt[1], *heads[:2], inv), 18 * plan.rows_loc * SEP**2, 16 * plan.rows_loc * SEP,
    )


def parent_cols(plan, scal, panel, heads, cols, inv):
    count = plan.col_blocks

    def kernel(s, p_ref, th, tl, cah, cal, cbh, cbl, l_ref, hi_ref, lo_ref, lh, ll, rh, rl):
        j = pl.program_id(0)

        @pl.when(j == 0)
        def _():
            unpack(l_ref, 0, False, lh, ll)
            for k in (0, 1):
                keep = plan.source(s, k, 1) >= 0
                drop = (lax.broadcasted_iota(jnp.int32, (SEP, SEP), 0) >= BLK) & jnp.logical_not(keep)
                rh[k] = jnp.where(drop, 0.0, th[k].astype(F32)).astype(BF16)
                rl[k] = jnp.where(drop, 0.0, tl[k].astype(F32)).astype(BF16)

        value = p_ref[...]
        for k, (high, low) in enumerate(((cah, cal), (cbh, cbl))):
            valid, _ = plan.col_at(s, k, j)
            value = value - jnp.where(valid, dot3((rh[k], rl[k]), (high[...], low[...])), 0.0)
        hi_ref[...], lo_ref[...] = split(dot3((lh[...], ll[...]), split(value)))

    blk = (SEP, BLK)
    head = pl.BlockSpec((2, SEP, SEP), lambda j, s: (0, 0, 0))
    right = [pl.BlockSpec(blk, lambda j, s, k=k: (0, plan.col_at(s, k, j)[1])) for k in (0, 0, 1, 1)]
    out = pl.BlockSpec(blk, lambda j, s: (0, j))
    return call(
        kernel, (count,), [out] + [head] * 2 + right + [pl.BlockSpec((1, PACKED, DB), lambda j, s: (0, 0, 0))],
        [shape_of((SEP, plan.cols_loc), BF16)] * 2, [out, out],
        [pltpu.VMEM((SEP, SEP), BF16)] * 2 + [pltpu.VMEM((2, SEP, SEP), BF16)] * 2,
        (scal, panel, *heads[2:], *cols[0], *cols[1], inv),
        18 * plan.cols_loc * SEP**2, 16 * plan.cols_loc * SEP,
    )


def child_result(plan, scal, k, fronts, rt, cols, result):
    wide = plan.cols_loc

    def kernel(s, a_ref, lh, ll, rh, rl, *rest):
        out_ref = rest[-1]
        i = pl.program_id(0)
        top = (plan.r(s) == 0) & (i < GAP)

        @pl.when(top)
        def _():
            rows = pl.ds(pl.multiple_of(jnp.minimum(i, GAP - 1) * BLK, BLK), BLK)
            out_ref[0] = rh[rows, :].astype(F32) + rl[rows, :].astype(F32)

        @pl.when(jnp.logical_not(top))
        def _():
            out_ref[0] = a_ref[0] - dot3((lh[...], ll[...]), (rh[...], rl[...]))

            @pl.when(plan.c(s) == 0)
            def _():
                out_ref[0, :, pl.ds(0, SEP)] = jnp.zeros((BLK, SEP), F32)

    block = pl.BlockSpec((1, BLK, wide), lambda i, s: (k, i, 0))
    left = pl.BlockSpec((BLK, SEP), lambda i, s: (i, 0))
    right = pl.BlockSpec((SEP, wide), lambda i, s: (0, 0))
    extra_specs = [] if result is None else [pl.BlockSpec(memory_space=pl.ANY)]
    extra = [] if result is None else [result]
    return call(
        kernel, (plan.row_blocks,), [block, left, left, right, right] + extra_specs,
        shape_of(fronts.shape), block, [], (scal, fronts, *rt, *cols, *extra),
        6 * plan.rows_loc * wide * SEP, 8 * plan.rows_loc * wide,
        aliases={} if result is None else {6: 0},
    )


def edge_sum(plan, scal, fronts, after, first, count):
    last = plan.row_blocks - 1
    inner = after is None

    def kernel(s, a_ref, b_ref, *rest):
        out_ref = rest[-1]
        i = pl.program_id(0) + first
        for j in range(GAP):
            total = jnp.zeros((BLK, BLK), F32)
            for k, ref in enumerate((a_ref, b_ref)):
                valid_row, at_row = plan.row_at(s, k, i)
                valid_col, at_col = plan.before_at(s, k, j)
                lanes = pl.ds(pl.multiple_of(at_col * BLK, BLK), BLK)
                value = ref[0, :, lanes]
                if not inner:
                    value = jnp.where(at_row > last, rest[k][0, :, lanes], value)
                total = total + jnp.where(valid_row & valid_col, value, 0.0)
            out_ref[:, pl.ds(j * BLK, BLK)] = total

    blk = (1, BLK, SEP)
    own = [pl.BlockSpec(blk, lambda g, s, k=k: (k, jnp.minimum(plan.row_at(s, k, g + first)[1], last), 0)) for k in (0, 1)]
    ext = [
        pl.BlockSpec(blk, lambda g, s, k=k: (k, jnp.clip(plan.row_at(s, k, g + first)[1] - last - 1, 0, GAP - 1), 0))
        for k in (0, 1)
    ]
    return call(
        kernel, (count,), own + ([] if inner else ext), shape_of((count * BLK, SEP)),
        pl.BlockSpec((BLK, SEP), lambda g, s: (g, 0)), [],
        (scal, fronts, fronts) + (() if inner else (after, after)), 1e6, 16 * count * BLK * SEP,
    )


def add_entries(plan, s, i, total_ref, refs, ext_refs, edge_ref, out_wide):
    last = plan.row_blocks - 1
    for k in (0, 1):
        valid_row, at_row = plan.row_at(s, k, i)
        for j in range(plan.col_blocks):
            valid_col, at_col = plan.col_at(s, k, j)
            here = valid_row & valid_col & (at_col < plan.col_blocks)

            @pl.when(here)
            def _(k=k, j=j, at_col=at_col, at_row=at_row):
                lanes = pl.ds(pl.multiple_of(at_col * BLK, BLK), BLK)
                value = refs[k][0, :, lanes]
                if ext_refs is not None:
                    value = jnp.where(at_row > last, ext_refs[k][0, :, lanes], value)
                total_ref[:, pl.ds(j * BLK, BLK)] += value

    @pl.when(plan.c(s) < plan.cols - 1)
    def _():
        total_ref[:, pl.ds(out_wide - SEP, SEP)] += edge_ref[...]


def panel_start(plan, scal, entries, fronts, edge):
    wide = plan.cols_loc

    def kernel(s, e_ref, a_ref, b_ref, x_ref, out_ref):
        out_ref[...] = e_ref[...]
        add_entries(plan, s, pl.program_id(0), out_ref, (a_ref, b_ref), None, x_ref, wide)

    blk = (BLK, wide)
    own = [
        pl.BlockSpec((1, BLK, wide), lambda g, s, k=k: (k, plan.row_at(s, k, g)[1], 0)) for k in (0, 1)
    ]
    here = pl.BlockSpec(blk, lambda g, s: (g, 0))
    return call(
        kernel, (GAP,), [here] + own + [pl.BlockSpec((BLK, SEP), lambda g, s: (g, 0))],
        shape_of((SEP, wide)), here, [], (scal, entries, fronts, fronts, edge), 1e6, 16 * SEP * wide,
    )


def parent_result(plan, scal, entries, fronts, after, edge_top, edge_rest, rt, cols, prt, pcols):
    wide = plan.cols_loc
    last = plan.row_blocks - 1
    lhs_blk = (BLK, SEP)

    def kernel(s, e_ref, a_ref, b_ref, xa_ref, xb_ref, t_ref, u_ref, ah, al, bh, bl, ph, pll, cah, cal, cbh, cbl,
               qh, ql, out_ref, rh, rl, edge):
        i = pl.program_id(0)
        top = (plan.r(s) == 0) & (i < GAP)

        @pl.when(i == 0)
        def _():
            for k, (high, low) in enumerate(((cah, cal), (cbh, cbl))):
                for j in range(plan.col_blocks):
                    valid, at = plan.col_at(s, k, j)
                    lanes = pl.ds(pl.multiple_of(at * BLK, BLK), BLK)
                    here = pl.ds(j * BLK, BLK)
                    rh[k, :, here] = jnp.where(valid, high[:, lanes].astype(F32), 0.0).astype(BF16)
                    rl[k, :, here] = jnp.where(valid, low[:, lanes].astype(F32), 0.0).astype(BF16)

        @pl.when(top)
        def _():
            rows = pl.ds(pl.multiple_of(jnp.minimum(i, GAP - 1) * BLK, BLK), BLK)
            out_ref[...] = qh[rows, :].astype(F32) + ql[rows, :].astype(F32)

        @pl.when(jnp.logical_not(top))
        def _():
            out_ref[...] = e_ref[...] - dot3((ph[...], pll[...]), (qh[...], ql[...]))
            for k, (high, low) in enumerate(((ah, al), (bh, bl))):
                valid, _ = plan.row_at(s, k, i)

                @pl.when(valid)
                def _(k=k, high=high, low=low):
                    out_ref[...] -= dot3((high[...], low[...]), (rh[k], rl[k]))

            edge[...] = jnp.where(i < GAP, t_ref[...], u_ref[...])
            add_entries(plan, s, i, out_ref, (a_ref, b_ref), (xa_ref, xb_ref), edge, wide)

            @pl.when(plan.c(s) == 0)
            def _():
                out_ref[:, pl.ds(0, SEP)] = jnp.zeros((BLK, SEP), F32)

    here = pl.BlockSpec((BLK, wide), lambda g, s: (g, 0))
    front = (1, BLK, wide)
    own = [pl.BlockSpec(front, lambda g, s, k=k: (k, jnp.minimum(plan.row_at(s, k, g)[1], last), 0)) for k in (0, 1)]
    ext = [
        pl.BlockSpec(front, lambda g, s, k=k: (k, jnp.clip(plan.row_at(s, k, g)[1] - last - 1, 0, GAP - 1), 0))
        for k in (0, 1)
    ]
    top_spec = pl.BlockSpec(lhs_blk, lambda g, s: (jnp.minimum(g, GAP - 1), 0))
    rest_spec = pl.BlockSpec(lhs_blk, lambda g, s: (jnp.maximum(g - GAP, 0), 0))
    rows = [pl.BlockSpec(lhs_blk, lambda g, s, k=k: (plan.row_at(s, k, g)[1], 0)) for k in (0, 0, 1, 1)]
    prow = pl.BlockSpec(lhs_blk, lambda g, s: (g, 0))
    right = pl.BlockSpec((SEP, wide + SEP), lambda g, s: (0, 0))
    pright = pl.BlockSpec((SEP, wide), lambda g, s: (0, 0))
    return call(
        kernel, (plan.row_blocks,),
        [here] + own + ext + [top_spec, rest_spec] + rows + [prow] * 2 + [right] * 4 + [pright] * 2,
        shape_of((plan.rows_loc, wide)), here,
        [pltpu.VMEM((2, SEP, wide), BF16)] * 2 + [pltpu.VMEM(lhs_blk, F32)],
        (scal, entries, fronts, fronts, after, after, edge_top, edge_rest, *rt[0], *rt[1], *prt, *cols[0], *cols[1], *pcols),
        18 * plan.rows_loc * wide * SEP, 24 * plan.rows_loc * wide,
    )


def send(plan, value, pairs):
    flat = [(a * plan.cols + b, c * plan.cols + d) for (a, b), (c, d) in pairs]
    return lax.ppermute(value, ("row", "col"), flat)


def grid_of(plan):
    return [(a, b) for a in range(plan.rows) for b in range(plan.cols)]


def row_stages(plan, r, value):
    stride = plan.rows // 2
    while stride:
        sent = send(plan, value, [((a, b), (a + stride, b)) for a, b in grid_of(plan) if a % (2 * stride) == 0])
        if stride > 1:
            value = jnp.where(r % (2 * stride) == stride, sent, value)
        stride //= 2
    return value, sent


def row_broadcast(plan, r, value):
    held, sent = row_stages(plan, r, value)
    return jnp.where(r % 2 == 1, sent, held)


def from_next_row(plan, value):
    return send(plan, value, [((a + 1, b), (a, b)) for a, b in grid_of(plan) if a + 1 < plan.rows])


def from_next_col(plan, value):
    return send(plan, value, [((a, b + 1), (a, b)) for a, b in grid_of(plan) if b + 1 < plan.cols])


def from_first(plan, r, c, value):
    strides, stride = [1], plan.cols // 2
    while stride > 1:
        strides.append(stride)
        stride //= 2
    held = [0]
    for stride in strides:
        sent = send(plan, value, [((0, b), (0, b + stride)) for b in held])
        new = [b + stride for b in held]
        take = c == new[0]
        for b in new[1:]:
            take = take | (c == b)
        value = jnp.where(take, sent, value)
        held = held + new
    return row_broadcast(plan, r, value)


def cut_panels(plan, panels):
    rows, place, axis = plan.rows, lax.axis_index("col") // 2, panels.ndim - 2
    at = [(place + d) % rows * plan.piece for d in range(rows)]
    return [lax.dynamic_slice_in_dim(panels, start, plan.piece, axis) for start in at]


def gather_rows(plan, parts):
    rows, mine = plan.rows, 0.0
    for d, part in enumerate(parts):
        pairs = [((0, b), (b // 2, (b // 2 + d) % rows * 2 + b % 2)) for b in range(plan.cols)]
        mine = mine + send(plan, part, pairs)
    gathered = lax.all_gather(mine, "col", axis=0, tiled=False)
    return gathered.reshape((rows, 2) + mine.shape)


def local(plan, child_fronts, parent_entries, block_map):
    r, c = lax.axis_index("row"), lax.axis_index("col")
    slots = jnp.arange(block_map.shape[1], dtype=jnp.int32)[None, None, :] + GAP
    targets = jnp.arange(plan.blocks, dtype=jnp.int32)[None, :, None]
    source = jnp.max(jnp.where(block_map[:, None, :] == targets, slots, -1), axis=2)
    scal = jnp.concatenate([source.reshape(-1), jnp.stack([r, c]).astype(jnp.int32)])

    top = child_fronts[:, :SEP, :]
    parts = cut_panels(plan, jnp.swapaxes(top, 1, 2))
    rows = gather_rows(plan, parts)
    pivots = from_first(plan, r, c, pack_pivots(plan, scal, child_fronts, parts))
    edge_top = from_next_col(plan, edge_sum(plan, scal, child_fronts, None, 0, GAP))
    after_rows = from_next_row(plan, top)
    next_cols = send(plan, top[:, :, :SEP], [((0, b + 1), (0, b)) for b in range(plan.cols - 1)])
    wide = jnp.concatenate([top, next_cols], axis=2)
    panel = panel_start(plan, scal, parent_entries, child_fronts, edge_top)
    parent_parts = cut_panels(plan, panel.T)

    inv = child_factor(plan, scal, pivots, (wide, *parent_parts))
    parent_lines = gather_rows(plan, parent_parts)
    pinv = from_first(plan, r, c, parent_factor(plan, scal, panel, wide, inv, ()))

    held, sent = row_stages(plan, r, wide)
    panel = row_broadcast(plan, r, panel)
    slots = SEP // plan.piece
    second = divmod(1, plan.half)
    second = (second[1], second[0])
    head = row_broadcast(plan, r, rows[second[0] * slots : (second[0] + 1) * slots, second[1]])
    next_rows = from_next_row(plan, rows[:slots, 0])

    edge_rest = from_next_col(
        plan, edge_sum(plan, scal, child_fronts, after_rows, GAP, plan.row_blocks - GAP)
    )

    rt = [child_rows(plan, scal, k, rows, next_rows, inv) for k in (0, 1)]
    cols = [child_cols(plan, scal, k, held, sent, inv) for k in (0, 1)]
    heads = child_heads(plan, scal, head, inv)
    result = child_result(plan, scal, 0, child_fronts, rt[0], cols[0], None)
    result = child_result(plan, scal, 1, child_fronts, rt[1], cols[1], result)

    prt = parent_rows(plan, scal, parent_lines, rt, heads, pinv)
    pcols = parent_cols(plan, scal, panel, heads, cols, pinv)
    parent = parent_result(
        plan, scal, parent_entries, child_fronts, after_rows, edge_top, edge_rest, rt, cols, prt, pcols
    )
    return (result, parent)


def solution(mesh):
    placed = (P(None, "row", "col"), P("row", "col"), P())

    def run(child_fronts, parent_entries, block_map):
        plan = Plan(mesh.shape["row"], mesh.shape["col"], child_fronts.shape[1], child_fronts.shape[2])
        return local(plan, child_fronts, parent_entries, block_map)

    return jax.shard_map(
        run,
        mesh=mesh,
        in_specs=placed,
        out_specs=(P(None, "row", "col"), P("row", "col")),
        check_vma=False,
    )
```

```python
import jax
import jax.numpy as jnp
from jax import lax
from jax.experimental import pallas as pl
from jax.experimental.pallas import tpu as pltpu
from jax.sharding import PartitionSpec as P

SEP = 512
BLK = 256
GAP = SEP // BLK
DB = 128
SUB = 8
VMEM = 56 * 2**20
F32 = jnp.float32
BF16 = jnp.bfloat16


def split(value):
    high = value.astype(BF16)
    return high, (value - high.astype(F32)).astype(BF16)


def dot(a, b, dims=((1,), (0,)), precision=None):
    return lax.dot_general(a, b, (dims, ((), ())), precision=precision, preferred_element_type=F32)


def dot3(a, b, dims=((1,), (0,))):
    return dot(a[0], b[0], dims) + (dot(a[0], b[1], dims) + dot(a[1], b[0], dims))


def dot_full(a, b, dims=((1,), (0,))):
    return dot(a, b, dims, lax.Precision.HIGHEST)


def factor_diag(tiles):
    shape = tiles[0][0].shape
    sub_iota = lax.broadcasted_iota(jnp.int32, shape, 1)
    left = [tile[0] for tile in tiles]
    right = [tile[1] for tile in tiles]
    done = []

    def row(tile, k):
        return jnp.broadcast_to(tile[:, k : k + 1, :], shape)

    for t in range(len(tiles)):
        first = t * SUB

        def lanes(tile, k, first=first):
            return jnp.broadcast_to(tile[:, :, first + k : first + k + 1], shape)

        cols = [lanes(left[t], k) for k in range(SUB)]
        a = [[row(cols[k], i) for k in range(i + 1)] for i in range(SUB)]
        inv = [None] * SUB
        low = [[None] * SUB for _ in range(SUB)]
        for j in range(SUB):
            inv[j] = lax.rsqrt(a[j][j])
            for i in range(j + 1, SUB):
                low[i][j] = a[i][j] * inv[j]
            for i in range(j + 1, SUB):
                for k in range(j + 1, i + 1):
                    a[i][k] = a[i][k] - low[i][j] * low[k][j]
        m = [[None] * SUB for _ in range(SUB)]
        for j in range(SUB):
            m[j][j] = inv[j]
            for i in range(j + 1, SUB):
                total = low[i][j] * m[j][j]
                for k in range(j + 1, i):
                    total = total + low[i][k] * m[k][j]
                m[i][j] = -inv[i] * total
        mcol = []
        for k in range(SUB):
            vec = jnp.zeros(shape, F32)
            for i in range(k, SUB):
                vec = jnp.where(sub_iota == i, m[i][k], vec)
            mcol.append(vec)
        new_left = mcol[0] * row(left[t], 0)
        new_right = mcol[0] * row(right[t], 0)
        for k in range(1, SUB):
            new_left = new_left + mcol[k] * row(left[t], k)
            new_right = new_right + mcol[k] * row(right[t], k)
        done.append(new_right)
        rows_left = [row(new_left, i) for i in range(SUB)]
        rows_right = [row(new_right, i) for i in range(SUB)]
        for s in range(t + 1, len(tiles)):
            raw = [lanes(left[s], k) for k in range(SUB)]
            for i in range(SUB):
                g = m[i][0] * raw[0]
                for k in range(1, i + 1):
                    g = g + m[i][k] * raw[k]
                left[s] = left[s] - g * rows_left[i]
                right[s] = right[s] - g * rows_right[i]
    return done


def pack_at(i, j):
    return i * (i + 1) // 2 + j


PACKED = pack_at(SEP // DB, 0) * DB


def unpack(ref, b, transposed, high_ref, low_ref):
    for i in range(SEP // DB):
        for j in range(SEP // DB):
            at = (pl.ds(j * DB, DB), pl.ds(i * DB, DB)) if transposed else (pl.ds(i * DB, DB), pl.ds(j * DB, DB))
            if j <= i:
                block = ref[b, pl.ds(pack_at(i, j) * DB, DB), :]
                high_ref[at], low_ref[at] = split(block.T if transposed else block)
            else:
                high_ref[at] = low_ref[at] = jnp.zeros((DB, DB), BF16)


def chol_steps(work, diag, inv_ref):
    count = work.shape[0]
    steps = SEP // DB
    eye = (
        lax.broadcasted_iota(jnp.int32, (DB, DB), 0) == lax.broadcasted_iota(jnp.int32, (DB, DB), 1)
    ).astype(F32)
    for b in range(count):
        for k in range(steps):
            for j in range(steps):
                work[b, pl.ds(k * DB, DB), pl.ds(SEP + j * DB, DB)] = eye if j == k else jnp.zeros((DB, DB), F32)

    def step(k, carry):
        rows = pl.ds(pl.multiple_of(k * DB, DB), DB)
        for b in range(count):
            diag[b] = work[b, rows, rows]
        tiles = []
        for t in range(DB // SUB):
            unit = jnp.broadcast_to(eye[t * SUB : (t + 1) * SUB, :][None], (count, SUB, DB))
            tiles.append((diag[:, pl.ds(t * SUB, SUB), :], unit))
        outs = factor_diag(tiles)
        for t in range(DB // SUB):
            diag[:, pl.ds(t * SUB, SUB), :] = outs[t]
        for b in range(count):
            work[b, rows, :] = dot_full(diag[b], work[b, rows, :])

        def update(i, c):
            irows = pl.ds(pl.multiple_of(i * DB, DB), DB)
            for b in range(count):
                work[b, irows, :] = work[b, irows, :] - dot_full(work[b, rows, irows], work[b, rows, :], ((0,), (0,)))
            return c

        lax.fori_loop(k + 1, steps, update, 0)
        return carry

    lax.fori_loop(0, steps, step, 0)
    for b in range(count):
        for i in range(steps):
            for j in range(i + 1):
                inv_ref[b, pl.ds(pack_at(i, j) * DB, DB), :] = work[b, pl.ds(i * DB, DB), pl.ds(SEP + j * DB, DB)]


def call(kernel, grid, in_specs, out_shape, out_specs, scratch, args, flops, nbytes, aliases=None):
    return pl.pallas_call(
        kernel,
        out_shape=out_shape,
        grid_spec=pltpu.PrefetchScalarGridSpec(
            num_scalar_prefetch=1, grid=grid, in_specs=in_specs, out_specs=out_specs, scratch_shapes=scratch
        ),
        input_output_aliases=aliases or {},
        compiler_params=pltpu.CompilerParams(vmem_limit_bytes=VMEM),
        cost_estimate=pl.CostEstimate(flops=int(flops), bytes_accessed=int(nbytes), transcendentals=0),
    )(*args)


def shape_of(dims, dtype=F32):
    return jax.ShapeDtypeStruct(dims, dtype)


class Plan:
    def __init__(self, rows, cols, rows_loc, cols_loc):
        self.rows, self.cols, self.rows_loc, self.cols_loc = rows, cols, rows_loc, cols_loc
        self.row_blocks, self.col_blocks = rows_loc // BLK, cols_loc // BLK
        self.blocks = rows * rows_loc // BLK
        self.half = cols_loc // SEP
        self.piece = cols_loc // rows
        assert cols == 2 * rows and rows_loc == 2 * cols_loc and rows_loc >= 2 * SEP and cols_loc >= SEP

    def r(self, s):
        return s[2 * self.blocks]

    def c(self, s):
        return s[2 * self.blocks + 1]

    def source(self, s, k, block):
        return s[k * self.blocks + block]

    def row_at(self, s, k, i):
        found = self.source(s, k, self.r(s) * self.row_blocks + i)
        return found >= 0, jnp.where(found >= 0, found - self.r(s) * self.row_blocks, 0)

    def col_at(self, s, k, j):
        found = self.source(s, k, self.c(s) * self.col_blocks + j)
        return found >= 0, jnp.where(found >= 0, found - self.c(s) * self.col_blocks, 0)

    def before_at(self, s, k, j):
        start = self.c(s) * self.col_blocks
        found = self.source(s, k, jnp.maximum(start - GAP + j, 0)) - start
        valid = (found >= 0) & (start > 0)
        return valid, jnp.where(valid, found, 0)


def pack_pivots(plan, scal, fronts, ahead):
    def kernel(s, a_ref, *rest):
        out_ref = rest[-1]
        for k in (0, 1):
            for i in range(SEP // DB):
                for j in range(i, SEP // DB):
                    block = a_ref[k, pl.ds(i * DB, DB), pl.ds(j * DB, DB)]
                    out_ref[k, pl.ds(pack_at(j, i) * DB, DB), :] = block

    return call(
        kernel, (1,),
        [pl.BlockSpec((2, SEP, SEP), lambda g, s: (0, 0, 0))] + [pl.BlockSpec(memory_space=pl.ANY)] * len(ahead),
        shape_of((2, PACKED, DB)), pl.BlockSpec((2, PACKED, DB), lambda g, s: (0, 0, 0)), [],
        (scal, fronts, *ahead), 1, 4 * 2**20,
    )


def child_factor(plan, scal, pivots, ahead):
    def kernel(s, a_ref, *rest):
        inv_ref, work, diag = rest[-3:]
        for k in (0, 1):
            for i in range(SEP // DB):
                for j in range(SEP // DB):
                    at = (k, pl.ds(i * DB, DB), pl.ds(j * DB, DB))
                    zero = jnp.zeros((DB, DB), F32)
                    work[at] = a_ref[k, pl.ds(pack_at(j, i) * DB, DB), :] if j >= i else zero
        chol_steps(work, diag, inv_ref)

    block = pl.BlockSpec((2, PACKED, DB), lambda g, s: (0, 0, 0))
    return call(
        kernel, (1,), [block] + [pl.BlockSpec(memory_space=pl.ANY)] * len(ahead), shape_of((2, PACKED, DB)), block,
        [pltpu.VMEM((2, SEP, 2 * SEP), F32), pltpu.VMEM((2, DB, DB), F32)], (scal, pivots, *ahead), 4e10, 4 * 2**20,
    )


def parent_factor(plan, scal, panel, wide, inv, ahead):
    def kernel(s, m_ref, p_ref, l_ref, *rest):
        out_ref, work, diag, full = rest[-4:]
        first = (plan.r(s) == 0) & (plan.c(s) == 0)

        @pl.when(first)
        def _():
            steps = SEP // DB
            total = m_ref[...]
            for k in (0, 1):
                for i in range(steps):
                    for j in range(steps):
                        zero = jnp.zeros((DB, DB), F32)
                        block = l_ref[k, pl.ds(pack_at(i, j) * DB, DB), :] if j <= i else zero
                        full[pl.ds(i * DB, DB), pl.ds(j * DB, DB)] = block
                head = dot_full(full[...], p_ref[k])
                update = dot_full(head, head, ((0,), (0,)))
                keep = plan.source(s, k, 1) >= 0
                edge = lax.broadcasted_iota(jnp.int32, (SEP, SEP), 0) >= BLK
                edge = edge | (lax.broadcasted_iota(jnp.int32, (SEP, SEP), 1) >= BLK)
                total = total - jnp.where(edge & jnp.logical_not(keep), 0.0, update)
            work[0, :, pl.ds(0, SEP)] = total
            chol_steps(work, diag, out_ref)

        @pl.when(jnp.logical_not(first))
        def _():
            out_ref[...] = jnp.zeros(out_ref.shape, F32)

    both = pl.BlockSpec((2, PACKED, DB), lambda g, s: (0, 0, 0))
    return call(
        kernel, (1,),
        [pl.BlockSpec((SEP, SEP), lambda g, s: (0, 0)), pl.BlockSpec((2, SEP, SEP), lambda g, s: (0, 0, 1)), both]
        + [pl.BlockSpec(memory_space=pl.ANY)] * len(ahead),
        shape_of((1, PACKED, DB)), pl.BlockSpec((1, PACKED, DB), lambda g, s: (0, 0, 0)),
        [pltpu.VMEM((1, SEP, 2 * SEP), F32), pltpu.VMEM((1, DB, DB), F32), pltpu.VMEM((SEP, SEP), F32)],
        (scal, panel, wide, inv, *ahead), 4e10, 8 * 2**20,
    )


def child_rows(plan, scal, k, rows, after, inv):
    count = plan.rows_loc // SEP
    slots = SEP // plan.piece

    def kernel(s, o_ref, x_ref, l_ref, hi_ref, lo_ref, lh, ll):
        j = pl.program_id(0)

        @pl.when(j == 0)
        def _():
            unpack(l_ref, 0, True, lh, ll)

        value = jnp.where(j == count, x_ref[...].reshape(SEP, SEP), o_ref[...].reshape(SEP, SEP))
        hi_ref[...], lo_ref[...] = split(dot3(split(value), (lh[...], ll[...])))

    blk = (SEP, SEP)
    cut = (slots, 1, 1, plan.piece, SEP)
    out = pl.BlockSpec(blk, lambda j, s: (j, 0))

    def own_at(j, s):
        at = jnp.minimum(j, count - 1)
        return (at % plan.half, at // plan.half, k, 0, 0)

    return call(
        kernel, (count + 1,),
        [pl.BlockSpec(cut, own_at), pl.BlockSpec(cut[:1] + cut[2:], lambda j, s: (0, k, 0, 0)),
         pl.BlockSpec((1, PACKED, DB), lambda j, s: (k, 0, 0))],
        [shape_of(((count + 1) * SEP, SEP), BF16)] * 2, [out, out], [pltpu.VMEM(blk, BF16)] * 2,
        (scal, rows, after, inv), 6 * (count + 1) * SEP**3, 8 * (count + 1) * SEP**2,
    )


def child_heads(plan, scal, head, inv):
    slots = SEP // plan.piece

    def kernel(s, h_ref, l_ref, hi_ref, lo_ref, thi_ref, tlo_ref, lh, ll):
        unpack(l_ref, 0, False, lh, ll)
        value = split(h_ref[...].reshape(SEP, SEP))
        out = dot3((lh[...], ll[...]), value, ((1,), (1,)))
        hi_ref[0], lo_ref[0] = split(out)
        thi_ref[0], tlo_ref[0] = split(out.T)

    out = pl.BlockSpec((1, SEP, SEP), lambda k, s: (k, 0, 0))
    return call(
        kernel, (2,),
        [pl.BlockSpec((slots, 1, plan.piece, SEP), lambda k, s: (0, k, 0, 0)),
         pl.BlockSpec((1, PACKED, DB), lambda k, s: (k, 0, 0))],
        [shape_of((2, SEP, SEP), BF16)] * 4, [out] * 4, [pltpu.VMEM((SEP, SEP), BF16)] * 2,
        (scal, head, inv), 12 * SEP**3, 16 * SEP**2,
    )


def child_cols(plan, scal, k, held, sent, inv):
    count = plan.half + 1

    def kernel(s, h_ref, t_ref, l_ref, hi_ref, lo_ref, lh, ll):
        @pl.when(pl.program_id(0) == 0)
        def _():
            unpack(l_ref, 0, False, lh, ll)

        value = jnp.where(plan.r(s) % 2 == 1, t_ref[0], h_ref[0])
        hi_ref[...], lo_ref[...] = split(dot3((lh[...], ll[...]), split(value)))

    blk = (SEP, SEP)
    out = pl.BlockSpec(blk, lambda j, s: (0, j))
    return call(
        kernel, (count,),
        [pl.BlockSpec((1, SEP, SEP), lambda j, s: (k, 0, jnp.where(plan.r(s) % 2 == 1, 0, j))),
         pl.BlockSpec((1, SEP, SEP), lambda j, s: (k, 0, jnp.where(plan.r(s) % 2 == 1, j, 0))),
         pl.BlockSpec((1, PACKED, DB), lambda j, s: (k, 0, 0))],
        [shape_of((SEP, count * SEP), BF16)] * 2, [out, out], [pltpu.VMEM(blk, BF16)] * 2,
        (scal, held, sent, inv), 6 * count * SEP**3, 8 * count * SEP**2,
    )


def parent_rows(plan, scal, panel, rt, heads, inv):
    count = plan.row_blocks

    def kernel(s, o_ref, ah, al, bh, bl, ch, cl, l_ref, hi_ref, lo_ref, lh, ll, rh, rl):
        i = pl.program_id(0)

        @pl.when(i == 0)
        def _():
            unpack(l_ref, 0, True, lh, ll)
            for k in (0, 1):
                keep = plan.source(s, k, 1) >= 0
                drop = (lax.broadcasted_iota(jnp.int32, (SEP, SEP), 1) >= BLK) & jnp.logical_not(keep)
                rh[k] = jnp.where(drop, 0.0, ch[k].astype(F32)).astype(BF16)
                rl[k] = jnp.where(drop, 0.0, cl[k].astype(F32)).astype(BF16)

        value = o_ref[...].reshape(BLK, SEP)
        for k, (high, low) in enumerate(((ah, al), (bh, bl))):
            valid, _ = plan.row_at(s, k, i)
            value = value - jnp.where(valid, dot3((high[...], low[...]), (rh[k], rl[k])), 0.0)
        hi_ref[...], lo_ref[...] = split(dot3(split(value), (lh[...], ll[...])))

    blk = (BLK, SEP)
    slots = BLK // plan.piece
    in_panel = count // 2
    own = pl.BlockSpec((slots, 1, plan.piece, SEP), lambda i, s: (i % in_panel, i // in_panel, 0, 0))
    rows = [pl.BlockSpec(blk, lambda i, s, k=k: (plan.row_at(s, k, i)[1], 0)) for k in (0, 0, 1, 1)]
    head = pl.BlockSpec((2, SEP, SEP), lambda i, s: (0, 0, 0))
    out = pl.BlockSpec(blk, lambda i, s: (i, 0))
    return call(
        kernel, (count,), [own] + rows + [head] * 2 + [pl.BlockSpec((1, PACKED, DB), lambda i, s: (0, 0, 0))],
        [shape_of((plan.rows_loc, SEP), BF16)] * 2, [out, out],
        [pltpu.VMEM((SEP, SEP), BF16)] * 2 + [pltpu.VMEM((2, SEP, SEP), BF16)] * 2,
        (scal, panel, *rt[0], *rt[1], *heads[:2], inv), 18 * plan.rows_loc * SEP**2, 16 * plan.rows_loc * SEP,
    )


def parent_cols(plan, scal, panel, heads, cols, inv):
    count = plan.col_blocks

    def kernel(s, p_ref, th, tl, cah, cal, cbh, cbl, l_ref, hi_ref, lo_ref, lh, ll, rh, rl):
        j = pl.program_id(0)

        @pl.when(j == 0)
        def _():
            unpack(l_ref, 0, False, lh, ll)
            for k in (0, 1):
                keep = plan.source(s, k, 1) >= 0
                drop = (lax.broadcasted_iota(jnp.int32, (SEP, SEP), 0) >= BLK) & jnp.logical_not(keep)
                rh[k] = jnp.where(drop, 0.0, th[k].astype(F32)).astype(BF16)
                rl[k] = jnp.where(drop, 0.0, tl[k].astype(F32)).astype(BF16)

        value = p_ref[...]
        for k, (high, low) in enumerate(((cah, cal), (cbh, cbl))):
            valid, _ = plan.col_at(s, k, j)
            value = value - jnp.where(valid, dot3((rh[k], rl[k]), (high[...], low[...])), 0.0)
        hi_ref[...], lo_ref[...] = split(dot3((lh[...], ll[...]), split(value)))

    blk = (SEP, BLK)
    head = pl.BlockSpec((2, SEP, SEP), lambda j, s: (0, 0, 0))
    right = [pl.BlockSpec(blk, lambda j, s, k=k: (0, plan.col_at(s, k, j)[1])) for k in (0, 0, 1, 1)]
    out = pl.BlockSpec(blk, lambda j, s: (0, j))
    return call(
        kernel, (count,), [out] + [head] * 2 + right + [pl.BlockSpec((1, PACKED, DB), lambda j, s: (0, 0, 0))],
        [shape_of((SEP, plan.cols_loc), BF16)] * 2, [out, out],
        [pltpu.VMEM((SEP, SEP), BF16)] * 2 + [pltpu.VMEM((2, SEP, SEP), BF16)] * 2,
        (scal, panel, *heads[2:], *cols[0], *cols[1], inv),
        18 * plan.cols_loc * SEP**2, 16 * plan.cols_loc * SEP,
    )


def child_result(plan, scal, k, fronts, rt, cols, result):
    wide = plan.cols_loc

    def kernel(s, a_ref, lh, ll, rh, rl, *rest):
        out_ref = rest[-1]
        i = pl.program_id(0)
        top = (plan.r(s) == 0) & (i == 0)

        @pl.when(top)
        def _():
            out_ref[0] = rh[...].astype(F32) + rl[...].astype(F32)

        @pl.when(jnp.logical_not(top))
        def _():
            out_ref[0] = a_ref[0] - dot3((lh[...], ll[...]), (rh[...], rl[...]))

            @pl.when(plan.c(s) == 0)
            def _():
                out_ref[0, :, pl.ds(0, SEP)] = jnp.zeros((SEP, SEP), F32)

    block = pl.BlockSpec((1, SEP, wide), lambda i, s: (k, i, 0))
    left = pl.BlockSpec((SEP, SEP), lambda i, s: (i, 0))
    right = pl.BlockSpec((SEP, wide), lambda i, s: (0, 0))
    extra_specs = [] if result is None else [pl.BlockSpec(memory_space=pl.ANY)]
    extra = [] if result is None else [result]
    return call(
        kernel, (plan.rows_loc // SEP,), [block, left, left, right, right] + extra_specs,
        shape_of(fronts.shape), block, [], (scal, fronts, *rt, *cols, *extra),
        6 * plan.rows_loc * wide * SEP, 8 * plan.rows_loc * wide,
        aliases={} if result is None else {6: 0},
    )


def edge_sum(plan, scal, fronts, after, first, count):
    last = plan.row_blocks - 1
    inner = after is None

    def kernel(s, a_ref, b_ref, *rest):
        out_ref = rest[-1]
        i = pl.program_id(0) + first
        for j in range(GAP):
            total = jnp.zeros((BLK, BLK), F32)
            for k, ref in enumerate((a_ref, b_ref)):
                valid_row, at_row = plan.row_at(s, k, i)
                valid_col, at_col = plan.before_at(s, k, j)
                lanes = pl.ds(pl.multiple_of(at_col * BLK, BLK), BLK)
                value = ref[0, :, lanes]
                if not inner:
                    value = jnp.where(at_row > last, rest[k][0, :, lanes], value)
                total = total + jnp.where(valid_row & valid_col, value, 0.0)
            out_ref[:, pl.ds(j * BLK, BLK)] = total

    blk = (1, BLK, SEP)
    own = [pl.BlockSpec(blk, lambda g, s, k=k: (k, jnp.minimum(plan.row_at(s, k, g + first)[1], last), 0)) for k in (0, 1)]
    ext = [
        pl.BlockSpec(blk, lambda g, s, k=k: (k, jnp.clip(plan.row_at(s, k, g + first)[1] - last - 1, 0, GAP - 1), 0))
        for k in (0, 1)
    ]
    return call(
        kernel, (count,), own + ([] if inner else ext), shape_of((count * BLK, SEP)),
        pl.BlockSpec((BLK, SEP), lambda g, s: (g, 0)), [],
        (scal, fronts, fronts) + (() if inner else (after, after)), 1e6, 16 * count * BLK * SEP,
    )


def add_entries(plan, s, i, total_ref, refs, ext_refs, edge_ref, out_wide):
    last = plan.row_blocks - 1
    for k in (0, 1):
        valid_row, at_row = plan.row_at(s, k, i)
        for j in range(plan.col_blocks):
            valid_col, at_col = plan.col_at(s, k, j)
            here = valid_row & valid_col & (at_col < plan.col_blocks)

            @pl.when(here)
            def _(k=k, j=j, at_col=at_col, at_row=at_row):
                lanes = pl.ds(pl.multiple_of(at_col * BLK, BLK), BLK)
                value = refs[k][0, :, lanes]
                if ext_refs is not None:
                    value = jnp.where(at_row > last, ext_refs[k][0, :, lanes], value)
                total_ref[:, pl.ds(j * BLK, BLK)] += value

    @pl.when(plan.c(s) < plan.cols - 1)
    def _():
        total_ref[:, pl.ds(out_wide - SEP, SEP)] += edge_ref[...]


def panel_start(plan, scal, entries, fronts, edge):
    wide = plan.cols_loc

    def kernel(s, e_ref, a_ref, b_ref, x_ref, out_ref):
        out_ref[...] = e_ref[...]
        add_entries(plan, s, pl.program_id(0), out_ref, (a_ref, b_ref), None, x_ref, wide)

    blk = (BLK, wide)
    own = [
        pl.BlockSpec((1, BLK, wide), lambda g, s, k=k: (k, plan.row_at(s, k, g)[1], 0)) for k in (0, 1)
    ]
    here = pl.BlockSpec(blk, lambda g, s: (g, 0))
    return call(
        kernel, (GAP,), [here] + own + [pl.BlockSpec((BLK, SEP), lambda g, s: (g, 0))],
        shape_of((SEP, wide)), here, [], (scal, entries, fronts, fronts, edge), 1e6, 16 * SEP * wide,
    )


def parent_result(plan, scal, entries, fronts, after, edge_top, edge_rest, rt, cols, prt, pcols):
    wide = plan.cols_loc
    last = plan.row_blocks - 1
    lhs_blk = (BLK, SEP)

    def kernel(s, e_ref, a_ref, b_ref, xa_ref, xb_ref, t_ref, u_ref, ah, al, bh, bl, ph, pll, cah, cal, cbh, cbl,
               qh, ql, out_ref, rh, rl, edge):
        i = pl.program_id(0)
        top = (plan.r(s) == 0) & (i < GAP)

        @pl.when(i == 0)
        def _():
            for k, (high, low) in enumerate(((cah, cal), (cbh, cbl))):
                for j in range(plan.col_blocks):
                    valid, at = plan.col_at(s, k, j)
                    lanes = pl.ds(pl.multiple_of(at * BLK, BLK), BLK)
                    here = pl.ds(j * BLK, BLK)
                    rh[k, :, here] = jnp.where(valid, high[:, lanes].astype(F32), 0.0).astype(BF16)
                    rl[k, :, here] = jnp.where(valid, low[:, lanes].astype(F32), 0.0).astype(BF16)

        @pl.when(top)
        def _():
            rows = pl.ds(pl.multiple_of(jnp.minimum(i, GAP - 1) * BLK, BLK), BLK)
            out_ref[...] = qh[rows, :].astype(F32) + ql[rows, :].astype(F32)

        @pl.when(jnp.logical_not(top))
        def _():
            out_ref[...] = e_ref[...] - dot3((ph[...], pll[...]), (qh[...], ql[...]))
            for k, (high, low) in enumerate(((ah, al), (bh, bl))):
                valid, _ = plan.row_at(s, k, i)

                @pl.when(valid)
                def _(k=k, high=high, low=low):
                    out_ref[...] -= dot3((high[...], low[...]), (rh[k], rl[k]))

            edge[...] = jnp.where(i < GAP, t_ref[...], u_ref[...])
            add_entries(plan, s, i, out_ref, (a_ref, b_ref), (xa_ref, xb_ref), edge, wide)

            @pl.when(plan.c(s) == 0)
            def _():
                out_ref[:, pl.ds(0, SEP)] = jnp.zeros((BLK, SEP), F32)

    here = pl.BlockSpec((BLK, wide), lambda g, s: (g, 0))
    front = (1, BLK, wide)
    own = [pl.BlockSpec(front, lambda g, s, k=k: (k, jnp.minimum(plan.row_at(s, k, g)[1], last), 0)) for k in (0, 1)]
    ext = [
        pl.BlockSpec(front, lambda g, s, k=k: (k, jnp.clip(plan.row_at(s, k, g)[1] - last - 1, 0, GAP - 1), 0))
        for k in (0, 1)
    ]
    top_spec = pl.BlockSpec(lhs_blk, lambda g, s: (jnp.minimum(g, GAP - 1), 0))
    rest_spec = pl.BlockSpec(lhs_blk, lambda g, s: (jnp.maximum(g - GAP, 0), 0))
    rows = [pl.BlockSpec(lhs_blk, lambda g, s, k=k: (plan.row_at(s, k, g)[1], 0)) for k in (0, 0, 1, 1)]
    prow = pl.BlockSpec(lhs_blk, lambda g, s: (g, 0))
    right = pl.BlockSpec((SEP, wide + SEP), lambda g, s: (0, 0))
    pright = pl.BlockSpec((SEP, wide), lambda g, s: (0, 0))
    return call(
        kernel, (plan.row_blocks,),
        [here] + own + ext + [top_spec, rest_spec] + rows + [prow] * 2 + [right] * 4 + [pright] * 2,
        shape_of((plan.rows_loc, wide)), here,
        [pltpu.VMEM((2, SEP, wide), BF16)] * 2 + [pltpu.VMEM(lhs_blk, F32)],
        (scal, entries, fronts, fronts, after, after, edge_top, edge_rest, *rt[0], *rt[1], *prt, *cols[0], *cols[1], *pcols),
        18 * plan.rows_loc * wide * SEP, 24 * plan.rows_loc * wide,
    )


def send(plan, value, pairs):
    flat = [(a * plan.cols + b, c * plan.cols + d) for (a, b), (c, d) in pairs]
    return lax.ppermute(value, ("row", "col"), flat)


def grid_of(plan):
    return [(a, b) for a in range(plan.rows) for b in range(plan.cols)]


def row_stages(plan, r, value):
    stride = plan.rows // 2
    while stride:
        sent = send(plan, value, [((a, b), (a + stride, b)) for a, b in grid_of(plan) if a % (2 * stride) == 0])
        if stride > 1:
            value = jnp.where(r % (2 * stride) == stride, sent, value)
        stride //= 2
    return value, sent


def row_broadcast(plan, r, value):
    held, sent = row_stages(plan, r, value)
    return jnp.where(r % 2 == 1, sent, held)


def from_next_row(plan, value):
    return send(plan, value, [((a + 1, b), (a, b)) for a, b in grid_of(plan) if a + 1 < plan.rows])


def from_next_col(plan, value):
    return send(plan, value, [((a, b + 1), (a, b)) for a, b in grid_of(plan) if b + 1 < plan.cols])


def from_first(plan, r, c, value):
    strides, stride = [1], plan.cols // 2
    while stride > 1:
        strides.append(stride)
        stride //= 2
    held = [0]
    for stride in strides:
        sent = send(plan, value, [((0, b), (0, b + stride)) for b in held])
        new = [b + stride for b in held]
        take = c == new[0]
        for b in new[1:]:
            take = take | (c == b)
        value = jnp.where(take, sent, value)
        held = held + new
    return row_broadcast(plan, r, value)


def cut_panels(plan, panels):
    rows, place, axis = plan.rows, lax.axis_index("col") // 2, panels.ndim - 2
    at = [(place + d) % rows * plan.piece for d in range(rows)]
    return [lax.dynamic_slice_in_dim(panels, start, plan.piece, axis) for start in at]


def gather_rows(plan, parts):
    rows, mine = plan.rows, 0.0
    for d, part in enumerate(parts):
        pairs = [((0, b), (b // 2, (b // 2 + d) % rows * 2 + b % 2)) for b in range(plan.cols)]
        mine = mine + send(plan, part, pairs)
    gathered = lax.all_gather(mine, "col", axis=0, tiled=False)
    return gathered.reshape((rows, 2) + mine.shape)


def local(plan, child_fronts, parent_entries, block_map):
    r, c = lax.axis_index("row"), lax.axis_index("col")
    slots = jnp.arange(block_map.shape[1], dtype=jnp.int32)[None, None, :] + GAP
    targets = jnp.arange(plan.blocks, dtype=jnp.int32)[None, :, None]
    source = jnp.max(jnp.where(block_map[:, None, :] == targets, slots, -1), axis=2)
    scal = jnp.concatenate([source.reshape(-1), jnp.stack([r, c]).astype(jnp.int32)])

    top = child_fronts[:, :SEP, :]
    parts = cut_panels(plan, jnp.swapaxes(top, 1, 2))
    rows = gather_rows(plan, parts)
    pivots = from_first(plan, r, c, pack_pivots(plan, scal, child_fronts, parts[:1]))
    edge_top = from_next_col(plan, edge_sum(plan, scal, child_fronts, None, 0, GAP))
    after_rows = from_next_row(plan, top)
    next_cols = send(plan, top[:, :, :SEP], [((0, b + 1), (0, b)) for b in range(plan.cols - 1)])
    wide = jnp.concatenate([top, next_cols], axis=2)
    panel = panel_start(plan, scal, parent_entries, child_fronts, edge_top)
    parent_parts = cut_panels(plan, panel.T)

    inv = child_factor(plan, scal, pivots, (wide, parent_parts[0]))
    parent_lines = gather_rows(plan, parent_parts)
    pinv = from_first(plan, r, c, parent_factor(plan, scal, panel, wide, inv, ()))

    held, sent = row_stages(plan, r, wide)
    panel = row_broadcast(plan, r, panel)
    slots = SEP // plan.piece
    second = divmod(1, plan.half)
    second = (second[1], second[0])
    head = row_broadcast(plan, r, rows[second[0] * slots : (second[0] + 1) * slots, second[1]])
    next_rows = from_next_row(plan, rows[:slots, 0])

    edge_rest = from_next_col(
        plan, edge_sum(plan, scal, child_fronts, after_rows, GAP, plan.row_blocks - GAP)
    )

    rt = [child_rows(plan, scal, k, rows, next_rows, inv) for k in (0, 1)]
    cols = [child_cols(plan, scal, k, held, sent, inv) for k in (0, 1)]
    heads = child_heads(plan, scal, head, inv)
    result = child_result(plan, scal, 0, child_fronts, rt[0], cols[0], None)
    result = child_result(plan, scal, 1, child_fronts, rt[1], cols[1], result)

    prt = parent_rows(plan, scal, parent_lines, rt, heads, pinv)
    pcols = parent_cols(plan, scal, panel, heads, cols, pinv)
    parent = parent_result(
        plan, scal, parent_entries, child_fronts, after_rows, edge_top, edge_rest, rt, cols, prt, pcols
    )
    return (result, parent)


def solution(mesh):
    placed = (P(None, "row", "col"), P("row", "col"), P())

    def run(child_fronts, parent_entries, block_map):
        plan = Plan(mesh.shape["row"], mesh.shape["col"], child_fronts.shape[1], child_fronts.shape[2])
        return local(plan, child_fronts, parent_entries, block_map)

    return jax.shard_map(
        run,
        mesh=mesh,
        in_specs=placed,
        out_specs=(P(None, "row", "col"), P("row", "col")),
        check_vma=False,
    )
```
